256 devices in a mesh: group: 4 (over y_lo, core), blk: 64 (over z, x, y_hi).
Axes of the slice: x: 4, y: 4 (y_hi: 2, y_lo: 2; y = y_hi * 2 + y_lo), z: 8, core: 2. Of those that a mesh axis runs over, the one named last changes fastest.
Arguments:
- features: bfloat16 [8192, 2048], P('blk', 'group'), may hold values from -16 to 16
- weight: bfloat16 [2048, 256], P('group'), may hold values from -0.125 to 0.125
- queue: bfloat16 [131072, 256], P(('group', 'blk')), may hold values from -0.5 to 0.5, as said below
- fresh_keys: bfloat16 [8192, 256], P('blk'), may hold values from -0.3984375 to 0.3984375
- positives: int32 [8192], P('blk'), may hold values from 0 to 8191, each once
- write_slot: int32 [1], replicated, may hold values from 0 to 122880
Outputs:
- query_loss: float32 [8192], P('blk')
- weight_grad: float32 [2048, 256], P(('group', 'blk'))
- new_queue: bfloat16 [131072, 256], P(('group', 'blk'))
The draws below stay inside these ranges and needn't reach their ends.
Inputs may be any that keep to these rules, and one draw needn't show every extreme that they name: `queue`: scaled item keys.
All inputs are finite; a program needn't handle non-finite values.
Results may differ from the reference program's by a relative error of at most 0.003.
The reference program's roundings to bfloat16 on the way count: a program that leaves them out, or rounds other values in their place, can miss the bound.
Values may be sent and summed in bfloat16 or wider, within the bound.
A program may use at most 64 MiB of HBM per device.

```python
import math
import jax
import jax.numpy as jnp
from jax import lax

WIDTH = 256
FEATURES = 2048
SLOT_ROWS = 512
QUERIES = 8192
SLOTS = 131072


def draw_queue(key, part):
    key_scale = jax.random.fold_in(key, 11)
    key_entries = jax.random.fold_in(key, 12)
    key_assign = jax.random.fold_in(key, 14)
    key_centres = jax.random.fold_in(key, 15)
    key_device = jax.random.fold_in(key, 16)
    centre_count = 128
    root = math.sqrt(WIDTH)
    device_total = SLOTS // SLOT_ROWS
    device_scale = jnp.exp(jax.random.uniform(key_device, (device_total, 1, 1), jnp.float32, math.log(0.4), math.log(2.5)))
    device_scale = jnp.broadcast_to(device_scale, (device_total, SLOT_ROWS, 1)).reshape(SLOTS, 1)
    scales = jnp.exp(jax.random.uniform(key_scale, (SLOTS, 1), jnp.float32, math.log(0.25), math.log(2.5)))
    rising = 0.8 + 0.4 * jnp.arange(SLOTS, dtype=jnp.float32)[:, None] / SLOTS
    centres = jax.random.normal(key_centres, (centre_count, WIDTH), jnp.float32)
    centres = centres / jnp.sqrt(jnp.sum(centres * centres, axis=1, keepdims=True))
    assign = jax.random.randint(key_assign, (SLOTS,), 0, centre_count)
    members = jnp.take(centres, assign, axis=0)
    noise = jax.random.normal(key_entries, (SLOTS, WIDTH), jnp.float32) / root
    entries = 0.9 * members + 0.45 * noise
    entries = jnp.clip(entries * scales * rising * device_scale, -0.5, 0.5)
    return entries.astype(jnp.bfloat16)


def spiked(drawn, stream_key, source, target, blocks, factor):
    owner, partner = [(jnp.arange(drawn.shape[axis_at]) // (drawn.shape[axis_at] // blocks)).reshape([-1 if axis == axis_at else 1 for axis in range(drawn.ndim)]) for axis_at in (source, target)]
    chosen = jax.random.permutation(stream_key, blocks)[partner]
    strong = (owner == chosen) | (owner == (partner + blocks // 2) % blocks)
    return jnp.where(strong, factor * drawn, drawn)


def block_levels(rng, dims, shards, smallest, high):
    def one(dim, parts):
        heights = jax.random.uniform(jax.random.fold_in(jax.random.fold_in(rng, 6), dim), (parts,), jnp.float32, smallest / len(shards), high / len(shards))
        return jnp.repeat(jnp.exp(heights), dims[dim] // parts).reshape((-1,) + (1,) * (len(dims) - dim - 1))

    factor_of = one(*shards[0])
    for cut in shards[1:]:
        factor_of = factor_of * one(*cut)
    return factor_of


def normal_values(own_key, dims, scale, reach, pieces=(), kind=jnp.bfloat16):
    array = jax.random.normal(own_key, dims, jnp.float32) * scale
    if len(pieces) > 0:
        array = block_levels(own_key, dims, pieces, -0.22, 0.18) * array
    return jnp.clip(array, min=-reach, max=reach).astype(kind)


def gaussian_with(key, dims, width, limit, pieces, heavy, held_as=jnp.bfloat16):
    values = width * jax.random.normal(key, dims, jnp.float32)
    if pieces:
        values = values * block_levels(key, dims, pieces, -0.22, 0.18)
    return jnp.clip(spiked(values, jax.random.fold_in(key, 3), *heavy), -limit, limit).astype(held_as)


def setup_inputs(seed: int = 0) -> dict:
    arg_keys = jax.random.split(jax.random.key(seed), 7)
    features = gaussian_with(arg_keys[0], (QUERIES, FEATURES), 1.0, 16.0, ((0, 64), (1, 4)), (0, 1, 64, 4.0))
    weight = normal_values(arg_keys[1], (FEATURES, WIDTH), FEATURES ** -0.5, 0.125, ((0, 4),))
    queue = draw_queue(jax.random.fold_in(arg_keys[6], 71), 0)
    fresh_keys = normal_values(arg_keys[3], (QUERIES, WIDTH), 0.0625, 0.3984375, ((0, 64),))
    positives = jax.random.permutation(arg_keys[4], QUERIES).astype(jnp.int32)
    write_slot = jax.random.randint(arg_keys[5], (1,), 0, SLOTS - QUERIES + 1).astype(jnp.int32)
    return {"features": features, "weight": weight, "queue": queue, "fresh_keys": fresh_keys, "positives": positives, "write_slot": write_slot}


epsilon = 1e-06
inverse_sharpness_factor = 8.0

def reference(features, weight, queue, fresh_keys, positives, write_slot):
    projected = jnp.dot(features, weight, preferred_element_type=jnp.float32)
    length = jnp.sqrt(lax.optimization_barrier(jnp.sum(projected * projected, axis=1, keepdims=True)) + epsilon)
    unit_rows = projected / length
    query_rows = unit_rows.astype(jnp.bfloat16)
    block_rows = 8192 if SLOTS % 8192 == 0 else SLOTS
    key_blocks = queue.reshape(SLOTS // block_rows, block_rows, WIDTH)

    def score_step(carry, keys):
        numerator, denominator = carry
        similarity_matrix = jnp.dot(query_rows, keys.T, preferred_element_type=jnp.float32)
        exponentials = jnp.exp(inverse_sharpness_factor * similarity_matrix)
        denominator = denominator + lax.optimization_barrier(jnp.sum(exponentials, axis=1))
        numerator = numerator + jnp.dot(exponentials.astype(jnp.bfloat16), keys, preferred_element_type=jnp.float32)
        return ((numerator, denominator), None)
    start_sums = (jnp.zeros((QUERIES, WIDTH), jnp.float32), jnp.zeros((QUERIES,), jnp.float32))
    (numerator, denominator), _ = lax.scan(score_step, start_sums, key_blocks)
    paired_encodings = jnp.take(fresh_keys, positives, axis=0).astype(jnp.float32)
    pair_score = inverse_sharpness_factor * lax.optimization_barrier(jnp.sum(query_rows.astype(jnp.float32) * paired_encodings, axis=1))
    pair_weight = jnp.exp(pair_score)
    probability_mass = pair_weight + denominator
    query_loss = jnp.log(probability_mass) - pair_score
    query_derivative = inverse_sharpness_factor * ((pair_weight[:, None] * paired_encodings + numerator) / probability_mass[:, None] - paired_encodings)
    along = lax.optimization_barrier(jnp.sum(query_derivative * unit_rows, axis=1, keepdims=True))
    grad_projected = ((query_derivative - along * unit_rows) / length).astype(jnp.bfloat16)
    weight_grad = jnp.dot(features.T, grad_projected, preferred_element_type=jnp.float32)
    window_start = write_slot[0].astype(jnp.int32)
    new_queue = lax.dynamic_update_slice(queue, fresh_keys, (window_start, jnp.int32(0)))
    return (query_loss, weight_grad, new_queue)
```

```python
import functools
import math

import jax
import jax.numpy as jnp
from jax import lax
from jax.experimental import pallas as pl
from jax.experimental.pallas import tpu as pltpu
from jax.sharding import PartitionSpec as P

EPSILON = 1e-06
SHARP = 8.0
SHARP_LOG2E = SHARP * math.log2(math.e)

Z, X, Y, CORES = 8, 4, 4, 2
ROWS = 32
WIDTH = 256
SLOT_ROWS = 512
QUERIES = 8192
F32 = jnp.float32
BF16 = jnp.bfloat16
COPIES = 128


def lane_sums(e):
    d = e[:, 0:128]
    for i in range(1, e.shape[1] // 128):
        d = d + e[:, 128 * i : 128 * (i + 1)]
    return d


def kernel(
    features,
    weight,
    queue,
    fresh,
    positives,
    write_slot,
    loss_out,
    wgrad_out,
    queue_out,
    proj,
    proj_in,
    queries,
    keys,
    fresh_all,
    pos_all,
    pick_out,
    pick_in,
    feat_t,
    num_out,
    num_in,
    numz_out,
    numz_in,
    den_out,
    den_in,
    denz_out,
    denz_in,
    gp_all,
    loss_rows,
    loss_in,
    wg,
    wg_in,
    wgz_out,
    wgz_in,
    wgy_out,
    wgy_in,
    send_sem,
    recv_sem,
):
    g = lax.axis_index("group")
    b = lax.axis_index("blk")
    y_lo, c = g // 2, g % 2
    z, x, y_hi = b // 8, (b // 2) % 4, b % 2
    y = 2 * y_hi + y_lo
    me_col = y * 2 + c

    def device(zz, xx, yy, cc):
        return {"group": (yy % 2) * 2 + cc, "blk": zz * 8 + xx * 2 + yy // 2}

    started = []

    def send(src, dst, to):
        at = len(started)
        copy = pltpu.make_async_remote_copy(
            src_ref=src,
            dst_ref=dst,
            send_sem=send_sem.at[at],
            recv_sem=recv_sem.at[at],
            device_id=to,
            device_id_type=pl.DeviceIdType.MESH,
        )
        copy.start()
        started.append(copy)
        return copy

    column = [(dy, dc) for dy in (0, 1, 3, 2) for dc in (1, 0) if (dy, dc) != (0, 0)]
    z_order = (1, 7, 2, 6, 3, 5, 4)
    x_order = (1, 3, 2)

    barrier = pltpu.get_barrier_semaphore()
    peers = [device(z, x, (y + dy) % 4, (c + dc) % 2) for dy, dc in column]
    peers += [device((z + d) % 8, x, y, c) for d in z_order]
    peers += [device(z, (x + d) % 4, y, c) for d in x_order]
    for p in peers:
        pl.semaphore_signal(barrier, inc=1, device_id=p, device_id_type=pl.DeviceIdType.MESH)

    proj[...] = jnp.dot(features[...], weight[...], preferred_element_type=F32).reshape(
        4, ROWS, WIDTH
    )
    fresh_all[z, x] = fresh[pl.ds(pl.multiple_of(g * ROWS, ROWS), ROWS), :]
    pos_all[0] = jnp.broadcast_to(positives[...], (8, 128))
    keys[me_col] = queue[...]
    pl.semaphore_wait(barrier, len(peers))

    group_peers = []
    for s in (1, 2, 3):
        yy, cc = 2 * y_hi + (y_lo + s // 2) % 2, (c + s % 2) % 2
        group_peers.append((s, yy, cc))
    proj_copies = [
        send(proj.at[(yy % 2) * 2 + cc], proj_in.at[s - 1], device(z, x, yy, cc))
        for s, yy, cc in group_peers
    ]

    up, down = (y + 1) % 4, (y + 3) % 4
    far = (y + 2) % 4
    other = 1 - c
    to_up, to_down = device(z, x, up, c), device(z, x, down, c)
    to_other = device(z, x, y, other)
    mine = keys.at[me_col]
    key_up = send(queue, mine, to_up)
    key_down = send(queue, mine, to_down)
    key_other = send(queue, mine, to_other)
    pos_copy = send(pos_all.at[0], pos_all.at[1], device(z, x, far, c))

    for copy in proj_copies:
        copy.wait_recv()
    projected = proj[g] + proj_in[0] + proj_in[1] + proj_in[2]
    length = jnp.sqrt(jnp.sum(projected * projected, axis=1, keepdims=True) + EPSILON)
    unit = projected / length
    query = unit.astype(BF16)
    queries[x, z] = query
    own_q = queries.at[x, z]
    qz = {d: send(own_q, own_q, device((z + d) % 8, x, y, c)) for d in z_order}
    qx = {(d, 0): send(own_q, own_q, device(z, (x + d) % 4, y, c)) for d in x_order}
    own_f = fresh_all.at[z, x]
    fz = [send(own_f, own_f, device((z + d) % 8, x, y, c)) for d in z_order]
    feat_t[...] = features[...].T
    for d in z_order:
        qz[d].wait_recv()
        block = queries.at[x, (z + 8 - d) % 8]
        for e in x_order:
            qx[e, d] = send(block, block, device(z, (x + e) % 4, y, c))

    key_up.wait_recv()
    from_down = keys.at[down * 2 + c]
    half = SLOT_ROWS // 2
    low, high = pl.ds(0, half), pl.ds(half, half)
    far_low = send(from_down.at[low], from_down.at[low], to_up)
    down_other = send(from_down, from_down, to_other)
    key_down.wait_recv()
    from_up = keys.at[up * 2 + c]
    far_high = send(from_up.at[high], from_up.at[high], to_down)
    up_other = send(from_up, from_up, to_other)
    from_far = keys.at[far * 2 + c]
    far_low.wait_recv()
    far_low_other = send(from_far.at[low], from_far.at[low], to_other)
    far_high.wait_recv()
    far_high_other = send(from_far.at[high], from_far.at[high], to_other)
    for copy in (key_other, down_other, up_other, far_low_other, far_high_other):
        copy.wait_recv()

    diagonal = lax.broadcasted_iota(jnp.int32, (ROWS, 128), 0) == lax.broadcasted_iota(
        jnp.int32, (ROWS, 128), 1
    )

    def tile(xx):
        q = queries[xx].reshape(Z * ROWS, WIDTH)
        num = den = None
        for j in range(8):
            k = keys[j]
            s = lax.dot_general(q, k, (((1,), (1,)), ((), ())), preferred_element_type=F32)
            e = jnp.exp2(s * SHARP_LOG2E)
            part = jnp.dot(e.astype(BF16), k, preferred_element_type=F32)
            sums = lane_sums(e)
            num = part if num is None else num + part
            den = sums if den is None else den + sums
        column_sums = jnp.sum(den, axis=1, keepdims=True).reshape(Z, ROWS, 1)
        den_rows = jnp.sum(jnp.where(diagonal[None], column_sums, 0.0), axis=1)
        return num.reshape(Z, ROWS, WIDTH), den_rows

    num_copies, den_copies = [], []

    def foreign_tile(i):
        d = x_order[i]
        for dz in (0, *z_order):
            qx[d, dz].wait_recv()
        owner = (x + 4 - d) % 4
        num, den = tile(owner)
        num_out[i] = num.astype(BF16)
        den_out[i] = den
        to = device(z, owner, y, c)
        den_copies.append(send(den_out.at[i], den_in.at[i], to))
        num_copies.append(send(num_out.at[i], num_in.at[i], to))

    foreign_tile(0)
    for copy in fz:
        copy.wait_recv()
    fresh_line = fresh_all.at[:, x]
    fx = [send(fresh_line, fresh_line, device(z, (x + d) % 4, y, c)) for d in x_order]
    foreign_tile(1)
    foreign_tile(2)

    for copy in fx:
        copy.wait_recv()
    pos_copy.wait_recv()
    lanes = lax.broadcasted_iota(jnp.int32, (128, 128), 1)
    offset = me_col * ROWS
    held = fresh_all[...].reshape(Z * X * ROWS, WIDTH)
    for r in range(2):
        wanted = jnp.broadcast_to(pos_all[r, 0:1, :], (128, 128)).astype(F32).T
        hits = []
        for m in range(8):
            at = 128 * m + lanes
            key = (at // ROWS) * WIDTH + offset + at % ROWS
            hits.append(jnp.where(wanted == key.astype(F32), 1.0, 0.0).astype(BF16))
        found = jnp.dot(jnp.concatenate(hits, axis=1), held, preferred_element_type=F32)
        found = found.astype(BF16).reshape(4, ROWS, WIDTH)
        for gg in range(4):
            pick_out[((y_hi + r) % 2) * 4 + gg, 0] = found[gg]

    slot = write_slot[0]

    def window(gg, bb):
        first = (gg * 64 + bb) * SLOT_ROWS - slot
        cycle = lax.shift_right_arithmetic(first, 8)
        return first, jnp.clip(cycle, 0, QUERIES // 256 - 3)

    for target in range(8):
        _, cycle = window(target % 4, z * 8 + x * 2 + target // 4)
        for k in range(3):
            at = cycle + k
            pick_out[target, 1 + k] = fresh_all[lax.shift_right_arithmetic(at, 2), at & 3]
    picks = []
    for dy, dc in column:
        yy, cc = (y + dy) % 4, (c + dc) % 2
        picks.append(send(pick_out.at[yy * 2 + cc], pick_in.at[me_col], device(z, x, yy, cc)))
    pick_in[me_col] = pick_out[me_col]

    num, den = tile(x)
    for i in range(3):
        den_copies[i].wait_recv()
        den = den + den_in[i]
        num_copies[i].wait_recv()
        num = num + num_in[i].astype(F32)
    numz_out[...] = num.astype(BF16)
    denz_out[...] = jnp.broadcast_to(den[:, None, :], (Z, 8, 128))
    numz, denz = [], []
    for i, d in enumerate(z_order):
        zz = (z + d) % 8
        to = device(zz, x, y, c)
        denz.append(send(denz_out.at[zz], denz_in.at[i], to))
        numz.append(send(numz_out.at[zz], numz_in.at[i], to))

    for copy in picks:
        copy.wait_recv()
    first, cycle = window(g, b)
    arrived = pick_in[...].reshape(1024, WIDTH)
    j = lax.broadcasted_iota(jnp.int32, (1, 1024), 1)
    kind = (j // ROWS) % 4
    held_key = (cycle + kind - 1) * 256 + (j // 128) * ROWS + j % ROWS
    held_key = jnp.where(kind == 0, -SLOT_ROWS * 1024, held_key)
    t = first + lax.broadcasted_iota(jnp.int32, (SLOT_ROWS, 1), 0)
    for r in range(0, SLOT_ROWS, 128):
        rows = t[r : r + 128]
        hit = jnp.where(rows == held_key, 1.0, 0.0).astype(BF16)
        moved = jnp.dot(hit, arrived, preferred_element_type=F32)
        old = queue[r : r + 128, :].astype(F32)
        inside = (rows >= 0) & (rows < QUERIES)
        queue_out[r : r + 128, :] = jnp.where(inside, moved, old).astype(BF16)
    positive = pick_in[0, 0].astype(F32)
    for src in range(1, 8):
        positive = positive + pick_in[src, 0].astype(F32)
    score = SHARP * jnp.sum(query.astype(F32) * positive, axis=1, keepdims=True)
    weight_p = jnp.exp(score)

    numerator = numz_out[z].astype(F32)
    den_row = denz_out[z]
    for i in range(7):
        denz[i].wait_recv()
        den_row = den_row + denz_in[i]
        numz[i].wait_recv()
        numerator = numerator + numz_in[i].astype(F32)
    denominator = jnp.sum(
        jnp.where(diagonal, jnp.broadcast_to(den_row[0:1, :], (ROWS, 128)), 0.0),
        axis=1,
        keepdims=True,
    )
    mass = weight_p + denominator
    loss = jnp.log(mass) - score
    grad = SHARP * ((weight_p * positive + numerator) / mass - positive)
    along = jnp.sum(grad * unit, axis=1, keepdims=True)
    grad_projected = ((grad - along * unit) / length).astype(BF16)
    gp_all[g] = grad_projected
    place = lax.broadcasted_iota(jnp.int32, (ROWS, 128), 0) + g * ROWS == (
        lax.broadcasted_iota(jnp.int32, (ROWS, 128), 1)
    )
    loss_row = jnp.sum(jnp.where(place, loss, 0.0), axis=0, keepdims=True)
    loss_rows[...] = jnp.broadcast_to(loss_row, (8, 128))
    gps = [send(gp_all.at[g], gp_all.at[g], device(z, x, yy, cc)) for _, yy, cc in group_peers]
    losses = [
        send(loss_rows, loss_in.at[s - 1], device(z, x, yy, cc)) for s, yy, cc in group_peers
    ]
    for copy in gps:
        copy.wait_recv()
    wg[...] = jnp.dot(
        feat_t[...], gp_all[...].reshape(128, WIDTH), preferred_element_type=F32
    ).reshape(Z, X, 16, WIDTH)
    wgx = []
    for i, d in enumerate(x_order):
        xx = (x + d) % 4
        wgx.append(send(wg.at[:, xx], wg_in.at[i], device(z, xx, y, c)))
    for i, copy in enumerate(losses):
        copy.wait_recv()
    loss_out[...] = (loss_rows[...] + loss_in[0] + loss_in[1] + loss_in[2])[0:1, :]
    for copy in wgx:
        copy.wait_recv()
    wgz_out[...] = wg[:, x] + wg_in[0] + wg_in[1] + wg_in[2]
    wgz = []
    for i, d in enumerate(z_order):
        zz = (z + d) % 8
        wgz.append(send(wgz_out.at[zz], wgz_in.at[i], device(zz, x, y, c)))
    total = wgz_out[z]
    for i in range(7):
        wgz[i].wait_recv()
        total = total + wgz_in[i]
    wgy_out[...] = total.reshape(2, 8, WIDTH)
    wgy = send(wgy_out.at[1 - y_hi], wgy_in, device(z, x, far, c))
    wgy.wait_recv()
    wgrad_out[...] = wgy_out[y_hi] + wgy_in[...]

    for copy in started:
        copy.wait_send()


def local(features, weight, queue, fresh_keys, positives, write_slot):
    vmem = pl.BlockSpec(memory_space=pltpu.VMEM)
    loss, weight_grad, new_queue = pl.pallas_call(
        kernel,
        out_shape=(
            jax.ShapeDtypeStruct((1, 128), F32),
            jax.ShapeDtypeStruct((8, WIDTH), F32),
            jax.ShapeDtypeStruct((SLOT_ROWS, WIDTH), BF16),
        ),
        in_specs=[vmem] * 5 + [pl.BlockSpec(memory_space=pltpu.SMEM)],
        out_specs=(vmem, vmem, vmem),
        scratch_shapes=[
            pltpu.VMEM((4, ROWS, WIDTH), F32),
            pltpu.VMEM((3, ROWS, WIDTH), F32),
            pltpu.VMEM((X, Z, ROWS, WIDTH), BF16),
            pltpu.VMEM((8, SLOT_ROWS, WIDTH), BF16),
            pltpu.VMEM((Z, X, ROWS, WIDTH), BF16),
            pltpu.VMEM((2, 8, 128), jnp.int32),
            pltpu.VMEM((8, 4, ROWS, WIDTH), BF16),
            pltpu.VMEM((8, 4, ROWS, WIDTH), BF16),
            pltpu.VMEM((512, 128), BF16),
            pltpu.VMEM((3, Z, ROWS, WIDTH), BF16),
            pltpu.VMEM((3, Z, ROWS, WIDTH), BF16),
            pltpu.VMEM((Z, ROWS, WIDTH), BF16),
            pltpu.VMEM((7, ROWS, WIDTH), BF16),
            pltpu.VMEM((3, 8, 128), F32),
            pltpu.VMEM((3, 8, 128), F32),
            pltpu.VMEM((Z, 8, 128), F32),
            pltpu.VMEM((7, 8, 128), F32),
            pltpu.VMEM((4, ROWS, WIDTH), BF16),
            pltpu.VMEM((8, 128), F32),
            pltpu.VMEM((3, 8, 128), F32),
            pltpu.VMEM((Z, X, 16, WIDTH), F32),
            pltpu.VMEM((3, Z, 16, WIDTH), F32),
            pltpu.VMEM((Z, 16, WIDTH), F32),
            pltpu.VMEM((7, 16, WIDTH), F32),
            pltpu.VMEM((2, 8, WIDTH), F32),
            pltpu.VMEM((8, WIDTH), F32),
            pltpu.SemaphoreType.DMA((COPIES,)),
            pltpu.SemaphoreType.DMA((COPIES,)),
        ],
        compiler_params=pltpu.CompilerParams(
            collective_id=0, has_side_effects=True, vmem_limit_bytes=48 << 20
        ),
        name="retrieval_step",
    )(features, weight, queue, fresh_keys, positives.reshape(1, 128), write_slot)
    return loss.reshape(128), weight_grad, new_queue


def solution(mesh):
    in_specs = (
        P("blk", "group"),
        P("group", None),
        P(("group", "blk"), None),
        P("blk", None),
        P("blk"),
        P(),
    )
    out_specs = (P("blk"), P(("group", "blk"), None), P(("group", "blk"), None))
    return jax.shard_map(local, mesh=mesh, in_specs=in_specs, out_specs=out_specs, check_vma=False)
```

```python
import functools
import math

import jax
import jax.numpy as jnp
from jax import lax
from jax.experimental import pallas as pl
from jax.experimental.pallas import tpu as pltpu
from jax.sharding import PartitionSpec as P

EPSILON = 1e-06
SHARP = 8.0
SHARP_LOG2E = SHARP * math.log2(math.e)

Z, X, Y, CORES = 8, 4, 4, 2
ROWS = 32
WIDTH = 256
SLOT_ROWS = 512
QUERIES = 8192
F32 = jnp.float32
BF16 = jnp.bfloat16
COPIES = 128


def lane_sums(e):
    d = e[:, 0:128]
    for i in range(1, e.shape[1] // 128):
        d = d + e[:, 128 * i : 128 * (i + 1)]
    return d


def kernel(
    features_hbm,
    weight_hbm,
    queue_hbm,
    fresh_hbm,
    positives_hbm,
    write_slot,
    loss_out,
    wgrad_out,
    queue_out,
    features,
    weight,
    proj,
    proj_in,
    queries,
    keys,
    fresh_all,
    pos_row,
    pos_all,
    pick_out,
    pick_in,
    fill_out,
    fill_in,
    feat_t,
    num_own,
    num_out,
    num_in,
    numz_out,
    numz_in,
    den_own,
    den_out,
    den_in,
    denz_out,
    denz_in,
    gp_all,
    loss_rows,
    loss_in,
    wg,
    wg_out,
    wg_in,
    wgz_out,
    wgz_in,
    local_sem,
    send_sem,
    recv_sem,
):
    g = lax.axis_index("group")
    b = lax.axis_index("blk")
    y_lo, c = g // 2, g % 2
    z, x, y_hi = b // 8, (b // 2) % 4, b % 2
    y = 2 * y_hi + y_lo
    me_col = y * 2 + c

    loads = [
        pltpu.make_async_copy(src, dst, local_sem.at[i])
        for i, (src, dst) in enumerate(
            (
                (features_hbm, features),
                (weight_hbm, weight),
                (queue_hbm, keys.at[me_col]),
                (fresh_hbm.at[pl.ds(pl.multiple_of(g * ROWS, ROWS), ROWS)], fresh_all.at[z, x]),
                (positives_hbm, pos_row),
            )
        )
    ]
    for copy in loads:
        copy.start()

    def device(zz, xx, yy, cc):
        return {"group": (yy % 2) * 2 + cc, "blk": zz * 8 + xx * 2 + yy // 2}

    started = []

    def send(src, dst, to):
        at = len(started)
        copy = pltpu.make_async_remote_copy(
            src_ref=src,
            dst_ref=dst,
            send_sem=send_sem.at[at],
            recv_sem=recv_sem.at[at],
            device_id=to,
            device_id_type=pl.DeviceIdType.MESH,
        )
        copy.start()
        started.append(copy)
        return copy

    column = [(dy, dc) for dy in (0, 1, 3, 2) for dc in (1, 0) if (dy, dc) != (0, 0)]
    z_order = (1, 7, 2, 6, 3, 5, 4)
    x_order = (1, 3, 2)
    rect = [(dx, dy) for dx in (1, 3, 2, 0) for dy in (2, 0) if (dx, dy) != (0, 0)]

    barrier = pltpu.get_barrier_semaphore()
    peers = [device((z + d) % 8, x, y, c) for d in z_order]
    peers += [device(z, x, (y + dy) % 4, (c + dc) % 2) for dy, dc in column]
    peers += [device(z, (x + dx) % 4, (y + dy) % 4, c) for dx, dy in rect if dx]
    for p in peers:
        pl.semaphore_signal(barrier, inc=1, device_id=p, device_id_type=pl.DeviceIdType.MESH)

    for copy in loads:
        copy.wait()
    proj[...] = jnp.dot(features[...], weight[...], preferred_element_type=F32).reshape(
        4, ROWS, WIDTH
    )
    pos_all[0] = jnp.broadcast_to(pos_row[...], (8, 128))
    pl.semaphore_wait(barrier, len(peers))

    group_peers = []
    for s in (1, 2, 3):
        yy, cc = 2 * y_hi + (y_lo + s // 2) % 2, (c + s % 2) % 2
        group_peers.append((s, yy, cc))
    proj_copies = [
        send(proj.at[(yy % 2) * 2 + cc], proj_in.at[s - 1], device(z, x, yy, cc))
        for s, yy, cc in group_peers
    ]

    up, down = (y + 1) % 4, (y + 3) % 4
    far = (y + 2) % 4
    other = 1 - c
    to_up, to_down = device(z, x, up, c), device(z, x, down, c)
    to_other = device(z, x, y, other)
    half = SLOT_ROWS // 2

    def part(yy, h):
        return keys.at[yy * 2 + c, pl.ds(h * half, half)]

    def pass_on(yy, h, to):
        return send(part(yy, h), part(yy, h), to)

    up_low = pass_on(y, 0, to_up)
    down_high = pass_on(y, 1, to_down)
    key_other = [pass_on(y, h, to_other) for h in range(2)]
    up_high = pass_on(y, 1, to_up)
    down_low = pass_on(y, 0, to_down)
    pos_copy = send(pos_all.at[0], pos_all.at[1], device(z, x, far, c))

    for copy in proj_copies:
        copy.wait_recv()
    projected = proj[g] + proj_in[0] + proj_in[1] + proj_in[2]
    length = jnp.sqrt(jnp.sum(projected * projected, axis=1, keepdims=True) + EPSILON)
    unit = projected / length
    query = unit.astype(BF16)
    queries[x, z] = query
    own_q = queries.at[x, z]
    qz = {d: send(own_q, own_q, device((z + d) % 8, x, y, c)) for d in z_order}
    qx = {(d, 0): send(own_q, own_q, device(z, (x + d) % 4, y, c)) for d in x_order}
    own_f = fresh_all.at[z, x]
    fz = [send(own_f, own_f, device((z + d) % 8, x, y, c)) for d in z_order]
    feat_t[...] = features[...].T

    up_low.wait_recv()
    far_low = pass_on(down, 0, to_up)
    key_other.append(pass_on(down, 0, to_other))
    down_high.wait_recv()
    far_high = pass_on(up, 1, to_down)
    key_other.append(pass_on(up, 1, to_other))
    for d in z_order:
        qz[d].wait_recv()
        block = queries.at[x, (z + 8 - d) % 8]
        for e in x_order:
            qx[e, d] = send(block, block, device(z, (x + e) % 4, y, c))
    up_high.wait_recv()
    key_other.append(pass_on(down, 1, to_other))
    down_low.wait_recv()
    key_other.append(pass_on(up, 0, to_other))
    for copy in key_other:
        copy.wait_recv()

    diagonal = lax.broadcasted_iota(jnp.int32, (ROWS, 128), 0) == lax.broadcasted_iota(
        jnp.int32, (ROWS, 128), 1
    )

    def tile(xx, where, num=None, den=None):
        q = queries[xx].reshape(Z * ROWS, WIDTH)
        for j in where:
            k = keys[j]
            s = lax.dot_general(q, k, (((1,), (1,)), ((), ())), preferred_element_type=F32)
            e = jnp.exp2(s * SHARP_LOG2E)
            p = jnp.dot(e.astype(BF16), k, preferred_element_type=F32)
            sums = lane_sums(e)
            num = p if num is None else num + p
            den = sums if den is None else den + sums
        return num, den

    def den_rows(den):
        column_sums = jnp.sum(den, axis=1, keepdims=True).reshape(Z, ROWS, 1)
        return jnp.sum(jnp.where(diagonal[None], column_sums, 0.0), axis=1)

    num_own[...], den_own[...] = tile(x, [yy * 2 + cc for yy in (y, down, up) for cc in (0, 1)])
    far_low.wait_recv()
    far_other = [pass_on(far, 0, to_other)]
    far_high.wait_recv()
    far_other.append(pass_on(far, 1, to_other))

    num_copies, den_copies = [], []

    def foreign_tile(i):
        d = x_order[i]
        for dz in (0, *z_order):
            qx[d, dz].wait_recv()
        if i == 0:
            for copy in far_other:
                copy.wait_recv()
        owner = (x + 4 - d) % 4
        num, den = tile(owner, range(8))
        num_out[i] = num.astype(BF16).reshape(Z, ROWS, WIDTH)
        den_out[i] = den_rows(den)
        to = device(z, owner, y, c)
        den_copies.append(send(den_out.at[i], den_in.at[i], to))
        num_copies.append(send(num_out.at[i], num_in.at[i], to))

    for copy in fz:
        copy.wait_recv()
    fresh_line = fresh_all.at[:, x]
    fx = [send(fresh_line, fresh_line, device(z, (x + d) % 4, y, c)) for d in x_order]
    foreign_tile(0)
    foreign_tile(1)

    for copy in fx:
        copy.wait_recv()
    pos_copy.wait_recv()
    held = fresh_all[...].reshape(Z * X * ROWS, WIDTH)
    lane = lax.broadcasted_iota(jnp.int32, (128, 128), 1)
    first_key = (lax.shift_right_logical(lane, 5) * 256 + (lane & 31) + me_col * ROWS).astype(F32)
    for r in range(2):
        wanted = jnp.broadcast_to(pos_all[r, 0:1, :], (128, 128)).astype(F32).T - first_key
        hits = [jnp.where(wanted == 1024.0 * m, 1.0, 0.0).astype(BF16) for m in range(8)]
        found = jnp.dot(jnp.concatenate(hits, axis=1), held, preferred_element_type=F32)
        found = found.astype(BF16).reshape(4, ROWS, WIDTH)
        for gg in range(4):
            pick_out[((y_hi + r) % 2) * 4 + gg] = found[gg]
    picks = []
    for dy, dc in column:
        yy, cc = (y + dy) % 4, (c + dc) % 2
        picks.append(send(pick_out.at[yy * 2 + cc], pick_in.at[me_col], device(z, x, yy, cc)))
    pick_in[me_col] = pick_out[me_col]
    foreign_tile(2)

    num, den = tile(x, [far * 2, far * 2 + 1], num_own[...], den_own[...])
    num, den = num.reshape(Z, ROWS, WIDTH), den_rows(den)
    for i in range(3):
        den_copies[i].wait_recv()
        den = den + den_in[i]
        num_copies[i].wait_recv()
        num = num + num_in[i].astype(F32)
    numz_out[...] = num.astype(BF16)
    denz_out[...] = jnp.broadcast_to(den[:, None, :], (Z, 8, 128))
    numz, denz = [], []
    for i, d in enumerate(z_order):
        zz = (z + d) % 8
        to = device(zz, x, y, c)
        denz.append(send(denz_out.at[zz], denz_in.at[i], to))
        numz.append(send(numz_out.at[zz], numz_in.at[i], to))

    slot = write_slot[0]

    def window(gg, bb):
        first = (gg * 64 + bb) * SLOT_ROWS - slot
        return first, lax.shift_right_arithmetic(first, 8)

    for target in range(8):
        _, cycle = window(target % 4, z * 8 + x * 2 + target // 4)
        for k in range(3):
            at = jnp.clip(cycle + k, 0, QUERIES // 256 - 1)
            fill_out[target, k] = fresh_all[lax.shift_right_logical(at, 2), at & 3]
    fills = []
    for dy, dc in column:
        yy, cc = (y + dy) % 4, (c + dc) % 2
        to = device(z, x, yy, cc)
        fills.append(send(fill_out.at[yy * 2 + cc], fill_in.at[:, me_col], to))
    fill_in[:, me_col] = fill_out[me_col]

    for copy in picks:
        copy.wait_recv()
    positive = pick_in[0].astype(F32)
    for src in range(1, 8):
        positive = positive + pick_in[src].astype(F32)
    score = SHARP * jnp.sum(query.astype(F32) * positive, axis=1, keepdims=True)
    weight_p = jnp.exp(score)

    numerator = numz_out[z].astype(F32)
    den_row = denz_out[z]
    for i in range(7):
        denz[i].wait_recv()
        den_row = den_row + denz_in[i]
        numz[i].wait_recv()
        numerator = numerator + numz_in[i].astype(F32)
    denominator = jnp.sum(
        jnp.where(diagonal, jnp.broadcast_to(den_row[0:1, :], (ROWS, 128)), 0.0),
        axis=1,
        keepdims=True,
    )
    mass = weight_p + denominator
    grad = SHARP * ((weight_p * positive + numerator) / mass - positive)
    along = jnp.sum(grad * unit, axis=1, keepdims=True)
    grad_projected = ((grad - along * unit) / length).astype(BF16)
    gp_all[g] = grad_projected
    gps = [send(gp_all.at[g], gp_all.at[g], device(z, x, yy, cc)) for _, yy, cc in group_peers]
    loss = jnp.log(mass) - score
    place = lax.broadcasted_iota(jnp.int32, (ROWS, 128), 0) + g * ROWS == (
        lax.broadcasted_iota(jnp.int32, (ROWS, 128), 1)
    )
    loss_row = jnp.sum(jnp.where(place, loss, 0.0), axis=0, keepdims=True)
    loss_rows[...] = jnp.broadcast_to(loss_row, (8, 128))
    losses = [
        send(loss_rows, loss_in.at[s - 1], device(z, x, yy, cc)) for s, yy, cc in group_peers
    ]
    for copy in gps:
        copy.wait_recv()
    grads = jnp.dot(feat_t[...], gp_all[...].reshape(128, WIDTH), preferred_element_type=F32)
    grads = grads.reshape(Z, X, 2, 8, WIDTH)
    for xx in range(X):
        for h in range(2):
            block = grads[:, xx, h].reshape(Z * 8, WIDTH)
            wg[xx * 2 + h] = block
            wg_out[xx * 2 + h] = block.astype(BF16)
    wgx = []
    for i, (dx, dy) in enumerate(rect):
        xx, yy = (x + dx) % 4, (y + dy) % 4
        wgx.append(send(wg_out.at[xx * 2 + yy // 2], wg_in.at[i], device(z, xx, yy, c)))

    for copy in fills:
        copy.wait_recv()
    first, cycle = window(g, b)
    arrived = fill_in[...].reshape(768, WIDTH)
    row = lax.broadcasted_iota(jnp.int32, (128, 128), 0)
    apart = row - lane + (first - cycle * 256)
    hit = [jnp.where(apart == 128 * m, 1.0, 0.0).astype(BF16) for m in range(3)]
    hit = jnp.concatenate(hit, axis=1)
    place_of = lax.broadcasted_iota(jnp.int32, (128, WIDTH), 0) + first
    for r in range(0, SLOT_ROWS, 128):
        moved = jnp.dot(hit, arrived[r : r + 384], preferred_element_type=F32)
        old = keys[me_col, r : r + 128, :].astype(F32)
        inside = (place_of >= -r) & (place_of < QUERIES - r)
        queue_out[r : r + 128, :] = jnp.where(inside, moved, old).astype(BF16)
    for copy in losses:
        copy.wait_recv()
    loss_out[...] = (loss_rows[...] + loss_in[0] + loss_in[1] + loss_in[2])[0:1, :]

    sums = wg[x * 2 + y_hi]
    for i, copy in enumerate(wgx):
        copy.wait_recv()
        sums = sums + wg_in[i].astype(F32)
    wgz_out[...] = sums.reshape(Z, 8, WIDTH)
    wgz = []
    for i, d in enumerate(z_order):
        zz = (z + d) % 8
        wgz.append(send(wgz_out.at[zz], wgz_in.at[i], device(zz, x, y, c)))
    total = wgz_out[z]
    for i in range(7):
        wgz[i].wait_recv()
        total = total + wgz_in[i]
    wgrad_out[...] = total

    for copy in started:
        copy.wait_send()


def local(features, weight, queue, fresh_keys, positives, write_slot):
    vmem = pl.BlockSpec(memory_space=pltpu.VMEM)
    loss, weight_grad, new_queue = pl.pallas_call(
        kernel,
        out_shape=(
            jax.ShapeDtypeStruct((1, 128), F32),
            jax.ShapeDtypeStruct((8, WIDTH), F32),
            jax.ShapeDtypeStruct((SLOT_ROWS, WIDTH), BF16),
        ),
        in_specs=[pl.BlockSpec(memory_space=pltpu.HBM)] * 5
        + [pl.BlockSpec(memory_space=pltpu.SMEM)],
        out_specs=(vmem, vmem, vmem),
        scratch_shapes=[
            pltpu.VMEM((128, 512), BF16),
            pltpu.VMEM((512, WIDTH), BF16),
            pltpu.VMEM((4, ROWS, WIDTH), F32),
            pltpu.VMEM((3, ROWS, WIDTH), F32),
            pltpu.VMEM((X, Z, ROWS, WIDTH), BF16),
            pltpu.VMEM((8, SLOT_ROWS, WIDTH), BF16),
            pltpu.VMEM((Z, X, ROWS, WIDTH), BF16),
            pltpu.VMEM((1, 128), jnp.int32),
            pltpu.VMEM((2, 8, 128), jnp.int32),
            pltpu.VMEM((8, ROWS, WIDTH), BF16),
            pltpu.VMEM((8, ROWS, WIDTH), BF16),
            pltpu.VMEM((8, 3, ROWS, WIDTH), BF16),
            pltpu.VMEM((3, 8, ROWS, WIDTH), BF16),
            pltpu.VMEM((512, 128), BF16),
            pltpu.VMEM((Z * ROWS, WIDTH), F32),
            pltpu.VMEM((3, Z, ROWS, WIDTH), BF16),
            pltpu.VMEM((3, Z, ROWS, WIDTH), BF16),
            pltpu.VMEM((Z, ROWS, WIDTH), BF16),
            pltpu.VMEM((7, ROWS, WIDTH), BF16),
            pltpu.VMEM((Z * ROWS, 128), F32),
            pltpu.VMEM((3, 8, 128), F32),
            pltpu.VMEM((3, 8, 128), F32),
            pltpu.VMEM((Z, 8, 128), F32),
            pltpu.VMEM((7, 8, 128), F32),
            pltpu.VMEM((4, ROWS, WIDTH), BF16),
            pltpu.VMEM((8, 128), F32),
            pltpu.VMEM((3, 8, 128), F32),
            pltpu.VMEM((8, Z * 8, WIDTH), F32),
            pltpu.VMEM((8, Z * 8, WIDTH), BF16),
            pltpu.VMEM((7, Z * 8, WIDTH), BF16),
            pltpu.VMEM((Z, 8, WIDTH), F32),
            pltpu.VMEM((7, 8, WIDTH), F32),
            pltpu.SemaphoreType.DMA((5,)),
            pltpu.SemaphoreType.DMA((COPIES,)),
            pltpu.SemaphoreType.DMA((COPIES,)),
        ],
        compiler_params=pltpu.CompilerParams(
            collective_id=0, has_side_effects=True, vmem_limit_bytes=48 << 20
        ),
        name="retrieval_step",
    )(features, weight, queue, fresh_keys, positives.reshape(1, 128), write_slot)
    return loss.reshape(128), weight_grad, new_queue


def solution(mesh):
    in_specs = (
        P("blk", "group"),
        P("group", None),
        P(("group", "blk"), None),
        P("blk", None),
        P("blk"),
        P(),
    )
    out_specs = (P("blk"), P(("group", "blk"), None), P(("group", "blk"), None))
    return jax.shard_map(local, mesh=mesh, in_specs=in_specs, out_specs=out_specs, check_vma=False)
```

```python
import functools
import math

import jax
import jax.numpy as jnp
from jax import lax
from jax.experimental import pallas as pl
from jax.experimental.pallas import tpu as pltpu
from jax.sharding import PartitionSpec as P

EPSILON = 1e-06
SHARP = 8.0
SHARP_LOG2E = SHARP * math.log2(math.e)

Z, X, Y, CORES = 8, 4, 4, 2
ROWS = 32
WIDTH = 256
SLOT_ROWS = 512
QUERIES = 8192
F32 = jnp.float32
BF16 = jnp.bfloat16
COPIES = 47


def lane_sums(e):
    d = e[:, 0:128]
    for i in range(1, e.shape[1] // 128):
        d = d + e[:, 128 * i : 128 * (i + 1)]
    return d


def kernel(
    features_hbm,
    weight_hbm,
    queue_hbm,
    fresh_hbm,
    positives_hbm,
    write_slot,
    loss_out,
    wgrad_out,
    queue_out,
    features,
    weight,
    proj,
    proj_in,
    queries,
    keys,
    fresh_all,
    pos_row,
    pos_all,
    pick_out,
    pick_in,
    fill_out,
    fill_in,
    feat_t,
    num_own,
    num_out,
    num_in,
    num_far_out,
    num_far_in,
    num_sum_out,
    num_sum_in,
    numz_out,
    numz_in,
    den_own,
    den_out,
    den_in,
    den_far_out,
    den_far_in,
    den_sum_out,
    den_sum_in,
    denz_out,
    denz_in,
    gp_all,
    loss_rows,
    loss_in,
    wg,
    wg_out,
    wg_in,
    wgz_out,
    wgz_in,
    queue_new,
    loss_new,
    wgrad_new,
    local_sem,
    send_sem,
    recv_sem,
):
    g = lax.axis_index("group")
    b = lax.axis_index("blk")
    y_lo, c = g // 2, g % 2
    z, x, y_hi = b // 8, (b // 2) % 4, b % 2
    y = 2 * y_hi + y_lo
    me_col = y * 2 + c

    loads = [
        pltpu.make_async_copy(src, dst, local_sem.at[i])
        for i, (src, dst) in enumerate(
            (
                (features_hbm, features),
                (weight_hbm, weight),
                (queue_hbm, keys.at[me_col]),
                (fresh_hbm.at[pl.ds(pl.multiple_of(g * ROWS, ROWS), ROWS)], fresh_all.at[z, x]),
                (positives_hbm, pos_row),
            )
        )
    ]
    for copy in loads:
        copy.start()

    def device(zz, xx, yy, cc):
        return {"group": (yy % 2) * 2 + cc, "blk": zz * 8 + xx * 2 + yy // 2}

    groups = []

    class Group:
        def __init__(self, whole):
            self.at, self.whole, self.got = len(groups), whole, False
            groups.append(self)

        def copy(self, src, dst, to):
            return pltpu.make_async_remote_copy(
                src_ref=src,
                dst_ref=dst,
                send_sem=send_sem.at[self.at],
                recv_sem=recv_sem.at[self.at],
                device_id=to,
                device_id_type=pl.DeviceIdType.MESH,
            )

        def send(self, src, dst, to):
            self.copy(src, dst, to).start()

        def wait_recv(self):
            self.got = True
            self.copy(self.whole, self.whole, neighbour).wait_recv()

        def wait_send(self):
            self.copy(self.whole, self.whole, neighbour).wait_send()

    neighbour = device(z, x, y, 1 - c)

    def send(src, dst, to):
        group = Group(src)
        group.send(src, dst, to)
        return group

    column = [(dy, dc) for dy in (0, 1, 3, 2) for dc in (1, 0) if (dy, dc) != (0, 0)]
    z_order = (1, 7, 2, 6, 3, 5, 4)
    z_far = (4, 3, 5, 2, 6, 1, 7)
    rect = [(dx, dy) for dx in (2, 1, 3, 0) for dy in (2, 0) if (dx, dy) != (0, 0)]
    x_near, x_far = (x + 1) % 4, (x + 2) % 4
    x_back = (x + 3) % 4

    barrier = pltpu.get_barrier_semaphore()
    peers = [device((z + d) % 8, x, y, c) for d in z_far]
    peers += [device(z, x, (y + dy) % 4, (c + dc) % 2) for dy, dc in column]
    peers += [device(z, (x + dx) % 4, (y + dy) % 4, c) for dx, dy in rect if dx]
    for p in peers:
        pl.semaphore_signal(barrier, inc=1, device_id=p, device_id_type=pl.DeviceIdType.MESH)

    for copy in loads:
        copy.wait()
    proj[...] = jnp.dot(features[...], weight[...], preferred_element_type=F32).reshape(
        4, ROWS, WIDTH
    )
    pos_all[0] = jnp.broadcast_to(pos_row[...], (8, 128))
    pl.semaphore_wait(barrier, len(peers))

    group_peers = []
    for s in (1, 2, 3):
        yy, cc = 2 * y_hi + (y_lo + s // 2) % 2, (c + s % 2) % 2
        group_peers.append((s, yy, cc))
    proj_copies = Group(proj_in)
    for s, yy, cc in group_peers:
        proj_copies.send(proj.at[(yy % 2) * 2 + cc], proj_in.at[s - 1], device(z, x, yy, cc))

    own_f = fresh_all.at[z, x]
    fz = Group(fresh_all.at[pl.ds(0, 7), x])
    fresh_far = send(own_f, own_f, device(z, x_far, y, c))
    for d in z_order:
        fz.send(own_f, own_f, device((z + d) % 8, x, y, c))

    up, down = (y + 1) % 4, (y + 3) % 4
    far = (y + 2) % 4
    other = 1 - c
    to_up, to_down = device(z, x, up, c), device(z, x, down, c)
    to_other = device(z, x, y, other)
    half = SLOT_ROWS // 2

    def part(yy, h):
        return keys.at[yy * 2 + c, pl.ds(h * half, half)]

    def pass_on(yy, h, to):
        return send(part(yy, h), part(yy, h), to)

    up_low = pass_on(y, 0, to_up)
    down_high = pass_on(y, 1, to_down)
    key_other = [pass_on(y, h, to_other) for h in range(2)]
    up_high = pass_on(y, 1, to_up)
    down_low = pass_on(y, 0, to_down)
    pos_copy = send(pos_all.at[0], pos_all.at[1], device(z, x, far, c))

    proj_copies.wait_recv()
    projected = proj[g] + proj_in[0] + proj_in[1] + proj_in[2]
    length = jnp.sqrt(jnp.sum(projected * projected, axis=1, keepdims=True) + EPSILON)
    unit = projected / length
    query = unit.astype(BF16)
    queries[x, z] = query
    own_q = queries.at[x, z]
    qx = {d: Group(queries.at[x]) for d in (1, 3)}
    query_far = send(own_q, own_q, device(z, x_far, y, c))
    qz = {d: send(own_q, own_q, device((z + d) % 8, x, y, c)) for d in z_order}
    for d in (1, 3):
        qx[d].send(own_q, own_q, device(z, (x + d) % 4, y, c))
    fresh_far.wait_recv()
    block = fresh_all.at[z, x_far]
    fz_far = Group(fresh_all.at[pl.ds(0, 7), x])
    for d in z_order:
        fz_far.send(block, block, device((z + d) % 8, x, y, c))
    fz.wait_recv()
    fresh_line = fresh_all.at[:, x]
    fx = Group(fresh_all.at[:, pl.ds(0, 2)])
    for xx in (x_near, x_back):
        fx.send(fresh_line, fresh_line, device(z, xx, y, c))
    feat_t[...] = features[...].T

    up_low.wait_recv()
    far_low = pass_on(down, 0, to_up)
    key_other.append(pass_on(down, 0, to_other))
    down_high.wait_recv()
    far_high = pass_on(up, 1, to_down)
    key_other.append(pass_on(up, 1, to_other))
    query_far.wait_recv()
    block = queries.at[x_far, z]
    qz_far = Group(queries.at[x, pl.ds(0, 7)])
    for d in z_order:
        qz_far.send(block, block, device((z + d) % 8, x, y, c))
    for d in z_order:
        qz[d].wait_recv()
        block = queries.at[x, (z + 8 - d) % 8]
        for e in (1, 3):
            qx[e].send(block, block, device(z, (x + e) % 4, y, c))
    up_high.wait_recv()
    key_other.append(pass_on(down, 1, to_other))
    down_low.wait_recv()
    key_other.append(pass_on(up, 0, to_other))
    for copy in key_other:
        copy.wait_recv()

    diagonal = lax.broadcasted_iota(jnp.int32, (ROWS, 128), 0) == lax.broadcasted_iota(
        jnp.int32, (ROWS, 128), 1
    )

    def tile(xx, where, num=None, den=None):
        q = queries[xx].reshape(Z * ROWS, WIDTH)
        for j in where:
            k = keys[j]
            s = lax.dot_general(q, k, (((1,), (1,)), ((), ())), preferred_element_type=F32)
            e = jnp.exp2(s * SHARP_LOG2E)
            p = jnp.dot(e.astype(BF16), k, preferred_element_type=F32)
            sums = lane_sums(e)
            num = p if num is None else num + p
            den = sums if den is None else den + sums
        return num, den

    def den_rows(den):
        column_sums = jnp.sum(den, axis=1, keepdims=True).reshape(Z, ROWS, 1)
        return jnp.sum(jnp.where(diagonal[None], column_sums, 0.0), axis=1)

    num_own[...], den_own[...] = tile(x, [yy * 2 + cc for yy in (y, down, up) for cc in (0, 1)])
    far_low.wait_recv()
    far_other = [pass_on(far, 0, to_other)]
    far_high.wait_recv()
    far_other.append(pass_on(far, 1, to_other))

    fz_far.wait_recv()
    fx.wait_recv()
    pos_copy.wait_recv()
    held = fresh_all[...].reshape(Z * X * ROWS, WIDTH)
    lane = lax.broadcasted_iota(jnp.int32, (128, 128), 1)
    first_key = (lax.shift_right_logical(lane, 5) * 256 + (lane & 31) + me_col * ROWS).astype(F32)
    for r in range(2):
        wanted = jnp.broadcast_to(pos_all[r, 0:1, :], (128, 128)).astype(F32).T - first_key
        hits = [jnp.where(wanted == 1024.0 * m, 1.0, 0.0).astype(BF16) for m in range(8)]
        found = jnp.dot(jnp.concatenate(hits, axis=1), held, preferred_element_type=F32)
        found = found.astype(BF16).reshape(4, ROWS, WIDTH)
        for gg in range(4):
            pick_out[((y_hi + r) % 2) * 4 + gg] = found[gg]
    picks = Group(pick_in.at[pl.ds(0, 7)])
    for dy, dc in column:
        yy, cc = (y + dy) % 4, (c + dc) % 2
        picks.send(pick_out.at[yy * 2 + cc], pick_in.at[me_col], device(z, x, yy, cc))
    pick_in[me_col] = pick_out[me_col]

    slot = write_slot[0]

    def window(gg, bb):
        first = (gg * 64 + bb) * SLOT_ROWS - slot
        return first, lax.shift_right_arithmetic(first, 8)

    for target in range(8):
        _, cycle = window(target % 4, z * 8 + x * 2 + target // 4)
        for k in range(3):
            at = jnp.clip(cycle + k, 0, QUERIES // 256 - 1)
            fill_out[target, k] = fresh_all[lax.shift_right_logical(at, 2), at & 3]
    fills = Group(fill_in.at[:, pl.ds(0, 7)])
    for dy, dc in column:
        yy, cc = (y + dy) % 4, (c + dc) % 2
        to = device(z, x, yy, cc)
        fills.send(fill_out.at[yy * 2 + cc], fill_in.at[:, me_col], to)
    fill_in[:, me_col] = fill_out[me_col]

    for copy in far_other:
        copy.wait_recv()
    num_copies, den_copies = [], []
    for i, d in enumerate((1, 3)):
        qx[d].wait_recv()
        owner = (x + 4 - d) % 4
        num, den = tile(owner, range(8))
        num_out[i] = num.astype(BF16).reshape(Z, ROWS, WIDTH)
        den_out[i] = den_rows(den)
        to = device(z, owner, y, c)
        den_copies.append(send(den_out.at[i], den_in.at[i], to))
        num_copies.append(send(num_out.at[i], num_in.at[i], to))
    qz_far.wait_recv()
    num, den = tile(x_far, range(8))
    num_far_out[...] = num.astype(BF16).reshape(Z, ROWS, WIDTH)
    den_far_out[...] = den_rows(den).reshape(Z, 1, 128)
    numf, denf = Group(num_far_in), Group(den_far_in)
    for i, d in enumerate(z_far):
        zz = (z + d) % 8
        to = device(zz, x, y, c)
        denf.send(den_far_out.at[zz], den_far_in.at[i], to)
        numf.send(num_far_out.at[zz], num_far_in.at[i], to)

    num, den = tile(x, [far * 2, far * 2 + 1], num_own[...], den_own[...])
    num, den = num.reshape(Z, ROWS, WIDTH), den_rows(den)
    for i in range(2):
        den_copies[i].wait_recv()
        den = den + den_in[i]
        num_copies[i].wait_recv()
        num = num + num_in[i].astype(F32)
    numz_out[...] = num.astype(BF16)
    denz_out[...] = den.reshape(Z, 1, 128)
    numz, denz = Group(numz_in), Group(denz_in)
    for i, d in enumerate(z_far):
        zz = (z + d) % 8
        to = device(zz, x, y, c)
        denz.send(denz_out.at[zz], denz_in.at[i], to)
        numz.send(numz_out.at[zz], numz_in.at[i], to)
    denf.wait_recv()
    numf.wait_recv()
    num, den = num_far_out[z].astype(F32), den_far_out[z]
    for i in range(7):
        num = num + num_far_in[i].astype(F32)
        den = den + den_far_in[i]
    num_sum_out[...] = num
    den_sum_out[...] = den
    to = device(z, x_far, y, c)
    den_sum = send(den_sum_out, den_sum_in, to)
    num_sum = send(num_sum_out, num_sum_in, to)

    picks.wait_recv()
    positive = pick_in[0].astype(F32)
    for src in range(1, 8):
        positive = positive + pick_in[src].astype(F32)
    score = SHARP * jnp.sum(query.astype(F32) * positive, axis=1, keepdims=True)
    weight_p = jnp.exp(score)

    numerator = numz_out[z].astype(F32)
    den_row = denz_out[z]
    denz.wait_recv()
    numz.wait_recv()
    for i in range(7):
        den_row = den_row + denz_in[i]
        numerator = numerator + numz_in[i].astype(F32)
    den_sum.wait_recv()
    den_row = den_row + den_sum_in[...]
    num_sum.wait_recv()
    numerator = numerator + num_sum_in[...]
    denominator = jnp.sum(
        jnp.where(diagonal, jnp.broadcast_to(den_row, (ROWS, 128)), 0.0),
        axis=1,
        keepdims=True,
    )
    mass = weight_p + denominator
    grad = SHARP * ((weight_p * positive + numerator) / mass - positive)
    along = jnp.sum(grad * unit, axis=1, keepdims=True)
    grad_projected = ((grad - along * unit) / length).astype(BF16)
    gp_all[g] = grad_projected
    gps = Group(gp_all.at[pl.ds(0, 3)])
    for _, yy, cc in group_peers:
        gps.send(gp_all.at[g], gp_all.at[g], device(z, x, yy, cc))
    loss = jnp.log(mass) - score
    place = lax.broadcasted_iota(jnp.int32, (ROWS, 128), 0) + g * ROWS == (
        lax.broadcasted_iota(jnp.int32, (ROWS, 128), 1)
    )
    loss_row = jnp.sum(jnp.where(place, loss, 0.0), axis=0, keepdims=True)
    loss_rows[...] = loss_row
    losses = Group(loss_in)
    for s, yy, cc in group_peers:
        losses.send(loss_rows, loss_in.at[s - 1], device(z, x, yy, cc))
    gps.wait_recv()
    grads = jnp.dot(feat_t[...], gp_all[...].reshape(128, WIDTH), preferred_element_type=F32)
    grads = grads.reshape(Z, X, 2, 8, WIDTH)
    for xx in range(X):
        for h in range(2):
            block = grads[:, xx, h].reshape(Z * 8, WIDTH)
            wg[xx * 2 + h] = block
            wg_out[xx * 2 + h] = block.astype(BF16)
    wgx = Group(wg_in)
    for i, (dx, dy) in enumerate(rect):
        xx, yy = (x + dx) % 4, (y + dy) % 4
        wgx.send(wg_out.at[xx * 2 + yy // 2], wg_in.at[i], device(z, xx, yy, c))

    fills.wait_recv()
    first, cycle = window(g, b)
    arrived = fill_in[...].reshape(768, WIDTH)
    row = lax.broadcasted_iota(jnp.int32, (128, 128), 0)
    apart = row - lane + (first - cycle * 256)
    hit = [jnp.where(apart == 128 * m, 1.0, 0.0).astype(BF16) for m in range(3)]
    hit = jnp.concatenate(hit, axis=1)
    place_of = lax.broadcasted_iota(jnp.int32, (128, WIDTH), 0) + first
    for r in range(0, SLOT_ROWS, 128):
        moved = jnp.dot(hit, arrived[r : r + 384], preferred_element_type=F32)
        old = keys[me_col, r : r + 128, :].astype(F32)
        inside = (place_of >= -r) & (place_of < QUERIES - r)
        queue_new[r : r + 128, :] = jnp.where(inside, moved, old).astype(BF16)
    stores = [pltpu.make_async_copy(queue_new, queue_out, local_sem.at[5])]
    stores[0].start()
    losses.wait_recv()
    loss_new[...] = loss_rows[...] + loss_in[0] + loss_in[1] + loss_in[2]
    stores.append(pltpu.make_async_copy(loss_new, loss_out, local_sem.at[6]))
    stores[1].start()

    sums = wg[x * 2 + y_hi]
    wgx.wait_recv()
    for i in range(7):
        sums = sums + wg_in[i].astype(F32)
    wgz_out[...] = sums.reshape(Z, 8, WIDTH)
    wgz = Group(wgz_in)
    for i, d in enumerate(z_far):
        zz = (z + d) % 8
        wgz.send(wgz_out.at[zz], wgz_in.at[i], device(zz, x, y, c))
    total = wgz_out[z]
    wgz.wait_recv()
    for i in range(7):
        total = total + wgz_in[i]
    wgrad_new[...] = total
    stores.append(pltpu.make_async_copy(wgrad_new, wgrad_out, local_sem.at[7]))
    stores[2].start()

    assert len(groups) == COPIES
    for group in groups:
        group.wait_send()
    for copy in stores:
        copy.wait()


def local(features, weight, queue, fresh_keys, positives, write_slot):
    hbm = pl.BlockSpec(memory_space=pltpu.HBM)
    loss, weight_grad, new_queue = pl.pallas_call(
        kernel,
        out_shape=(
            jax.ShapeDtypeStruct((1, 128), F32),
            jax.ShapeDtypeStruct((8, WIDTH), F32),
            jax.ShapeDtypeStruct((SLOT_ROWS, WIDTH), BF16),
        ),
        in_specs=[hbm] * 5 + [pl.BlockSpec(memory_space=pltpu.SMEM)],
        out_specs=(hbm, hbm, hbm),
        scratch_shapes=[
            pltpu.VMEM((128, 512), BF16),
            pltpu.VMEM((512, WIDTH), BF16),
            pltpu.VMEM((4, ROWS, WIDTH), F32),
            pltpu.VMEM((3, ROWS, WIDTH), F32),
            pltpu.VMEM((X, Z, ROWS, WIDTH), BF16),
            pltpu.VMEM((8, SLOT_ROWS, WIDTH), BF16),
            pltpu.VMEM((Z, X, ROWS, WIDTH), BF16),
            pltpu.VMEM((1, 128), jnp.int32),
            pltpu.VMEM((2, 8, 128), jnp.int32),
            pltpu.VMEM((8, ROWS, WIDTH), BF16),
            pltpu.VMEM((8, ROWS, WIDTH), BF16),
            pltpu.VMEM((8, 3, ROWS, WIDTH), BF16),
            pltpu.VMEM((3, 8, ROWS, WIDTH), BF16),
            pltpu.VMEM((512, 128), BF16),
            pltpu.VMEM((Z * ROWS, WIDTH), F32),
            pltpu.VMEM((2, Z, ROWS, WIDTH), BF16),
            pltpu.VMEM((2, Z, ROWS, WIDTH), BF16),
            pltpu.VMEM((Z, ROWS, WIDTH), BF16),
            pltpu.VMEM((7, ROWS, WIDTH), BF16),
            pltpu.VMEM((ROWS, WIDTH), F32),
            pltpu.VMEM((ROWS, WIDTH), F32),
            pltpu.VMEM((Z, ROWS, WIDTH), BF16),
            pltpu.VMEM((7, ROWS, WIDTH), BF16),
            pltpu.VMEM((Z * ROWS, 128), F32),
            pltpu.VMEM((2, 8, 128), F32),
            pltpu.VMEM((2, 8, 128), F32),
            pltpu.VMEM((Z, 1, 128), F32),
            pltpu.VMEM((7, 1, 128), F32),
            pltpu.VMEM((1, 128), F32),
            pltpu.VMEM((1, 128), F32),
            pltpu.VMEM((Z, 1, 128), F32),
            pltpu.VMEM((7, 1, 128), F32),
            pltpu.VMEM((4, ROWS, WIDTH), BF16),
            pltpu.VMEM((1, 128), F32),
            pltpu.VMEM((3, 1, 128), F32),
            pltpu.VMEM((8, Z * 8, WIDTH), F32),
            pltpu.VMEM((8, Z * 8, WIDTH), BF16),
            pltpu.VMEM((7, Z * 8, WIDTH), BF16),
            pltpu.VMEM((Z, 8, WIDTH), F32),
            pltpu.VMEM((7, 8, WIDTH), F32),
            pltpu.VMEM((SLOT_ROWS, WIDTH), BF16),
            pltpu.VMEM((1, 128), F32),
            pltpu.VMEM((8, WIDTH), F32),
            pltpu.SemaphoreType.DMA((8,)),
            pltpu.SemaphoreType.DMA((COPIES,)),
            pltpu.SemaphoreType.DMA((COPIES,)),
        ],
        compiler_params=pltpu.CompilerParams(
            collective_id=0, has_side_effects=True, vmem_limit_bytes=60 << 20
        ),
        name="retrieval_step",
    )(features, weight, queue, fresh_keys, positives.reshape(1, 128), write_slot)
    return loss.reshape(128), weight_grad, new_queue


def solution(mesh):
    in_specs = (
        P("blk", "group"),
        P("group", None),
        P(("group", "blk"), None),
        P("blk", None),
        P("blk"),
        P(),
    )
    out_specs = (P("blk"), P(("group", "blk"), None), P(("group", "blk"), None))
    return jax.shard_map(local, mesh=mesh, in_specs=in_specs, out_specs=out_specs, check_vma=False)
```

```python
import functools
import math

import jax
import jax.numpy as jnp
from jax import lax
from jax.experimental import pallas as pl
from jax.experimental.pallas import tpu as pltpu
from jax.sharding import PartitionSpec as P

EPSILON = 1e-06
SHARP = 8.0
SHARP_LOG2E = SHARP * math.log2(math.e)

Z, X, Y, CORES = 8, 4, 4, 2
ROWS = 32
WIDTH = 256
SLOT_ROWS = 512
QUERIES = 8192
F32 = jnp.float32
BF16 = jnp.bfloat16
COPIES = 41
LARGE, SMALL = 1043, 34


def lane_sums(e):
    d = e[:, 0:128]
    for i in range(1, e.shape[1] // 128):
        d = d + e[:, 128 * i : 128 * (i + 1)]
    return d


def kernel(
    features_hbm,
    weight_hbm,
    queue_hbm,
    fresh_hbm,
    positives_hbm,
    write_slot,
    loss_out,
    wgrad_out,
    queue_out,
    features,
    weight,
    proj,
    proj_in,
    queries,
    keys,
    fresh_all,
    pos_row,
    pos_all,
    pick_out,
    pick_in,
    fill_out,
    fill_in,
    feat_t,
    feat_z,
    num_own,
    num_out,
    num_in,
    num_far_out,
    num_far_in,
    num_sum_out,
    num_sum_in,
    numz_out,
    numz_in,
    den_own,
    den_out,
    den_in,
    den_far_out,
    den_far_in,
    den_sum_out,
    den_sum_in,
    den_line,
    denz_out,
    denz_in,
    gp_all,
    loss_rows,
    loss_in,
    wg,
    wgx_out,
    wgx_in,
    wgz_out,
    wgz_in,
    wgx2_out,
    wgx2_in,
    wgz2_out,
    wgz2_in,
    queue_new,
    loss_new,
    wgrad_new,
    sent_large,
    sent_small,
    local_sem,
    send_sem,
    recv_sem,
):
    g = lax.axis_index("group")
    b = lax.axis_index("blk")
    y_lo, c = g // 2, g % 2
    z, x, y_hi = b // 8, (b // 2) % 4, b % 2
    y = 2 * y_hi + y_lo
    me_col = y * 2 + c

    loads = [
        pltpu.make_async_copy(src, dst, local_sem.at[i])
        for i, (src, dst) in enumerate(
            (
                (features_hbm, features),
                (weight_hbm, weight),
                (queue_hbm, keys.at[me_col]),
                (fresh_hbm.at[pl.ds(pl.multiple_of(g * ROWS, ROWS), ROWS)], fresh_all.at[z, x]),
                (positives_hbm, pos_row),
            )
        )
    ]
    for copy in loads:
        copy.start()

    def device(zz, xx, yy, cc):
        return {"group": (yy % 2) * 2 + cc, "blk": zz * 8 + xx * 2 + yy // 2}

    groups, sent = [], [0, 0]

    def small(ref):
        return int(ref.shape[-2] == 1)

    class Group:
        def __init__(self, whole):
            self.at, self.whole, self.got = len(groups), whole, False
            groups.append(self)

        def copy(self, src, dst, to):
            return pltpu.make_async_remote_copy(
                src_ref=src,
                dst_ref=dst,
                send_sem=send_sem.at[small(src)],
                recv_sem=recv_sem.at[self.at],
                device_id=to,
                device_id_type=pl.DeviceIdType.MESH,
            )

        def send(self, src, dst, to):
            sent[small(src)] += math.prod(src.shape) * src.dtype.itemsize
            self.copy(src, dst, to).start()

        def wait_recv(self):
            self.got = True
            self.copy(self.whole, self.whole, neighbour).wait_recv()

    neighbour = device(z, x, y, 1 - c)

    def send(src, dst, to):
        group = Group(src)
        group.send(src, dst, to)
        return group

    column = [(dy, dc) for dy in (0, 1, 3, 2) for dc in (1, 0) if (dy, dc) != (0, 0)]
    z_order = (1, 7, 2, 6, 3, 5, 4)
    z_far = (4, 3, 5, 2, 6, 1, 7)
    z_line = (0, *z_order)
    rect = [(dx, dy) for dx in (2, 1, 3, 0) for dy in (2, 0) if (dx, dy) != (0, 0)]
    x_near, x_far = (x + 1) % 4, (x + 2) % 4
    x_back = (x + 3) % 4

    barrier = pltpu.get_barrier_semaphore()
    peers = [device((z + d) % 8, x, y, c) for d in z_far]
    peers += [device(z, x, (y + dy) % 4, (c + dc) % 2) for dy, dc in column]
    peers += [device(z, (x + dx) % 4, (y + dy) % 4, c) for dx, dy in rect if dx]
    for p in peers:
        pl.semaphore_signal(barrier, inc=1, device_id=p, device_id_type=pl.DeviceIdType.MESH)

    for copy in loads:
        copy.wait()
    proj[...] = jnp.dot(features[...], weight[...], preferred_element_type=F32).reshape(
        4, ROWS, WIDTH
    )
    pos_all[0] = jnp.broadcast_to(pos_row[...], (8, 128))
    pl.semaphore_wait(barrier, len(peers))

    group_peers = []
    for s in (1, 2, 3):
        yy, cc = 2 * y_hi + (y_lo + s // 2) % 2, (c + s % 2) % 2
        group_peers.append((s, yy, cc))
    proj_copies = Group(proj_in)
    for s, yy, cc in group_peers:
        proj_copies.send(proj.at[(yy % 2) * 2 + cc], proj_in.at[s - 1], device(z, x, yy, cc))

    own_f = fresh_all.at[z, x]
    fz = Group(fresh_all.at[pl.ds(0, 7), x])
    fresh_far = send(own_f, own_f, device(z, x_far, y, c))
    for d in z_order:
        fz.send(own_f, own_f, device((z + d) % 8, x, y, c))

    up, down = (y + 1) % 4, (y + 3) % 4
    far = (y + 2) % 4
    other = 1 - c
    to_up, to_down = device(z, x, up, c), device(z, x, down, c)
    to_other = device(z, x, y, other)
    half = SLOT_ROWS // 2

    def part(yy, h):
        return keys.at[yy * 2 + c, pl.ds(h * half, half)]

    def pass_on(yy, h, to):
        return send(part(yy, h), part(yy, h), to)

    up_low = pass_on(y, 0, to_up)
    down_high = pass_on(y, 1, to_down)
    key_other = Group(keys.at[pl.ds(0, 3)])
    for h in range(2):
        key_other.send(part(y, h), part(y, h), to_other)
    up_high = pass_on(y, 1, to_up)
    down_low = pass_on(y, 0, to_down)
    pos_copy = send(pos_all.at[0], pos_all.at[1], device(z, x, far, c))

    proj_copies.wait_recv()
    projected = proj[g] + proj_in[0] + proj_in[1] + proj_in[2]
    length = jnp.sqrt(jnp.sum(projected * projected, axis=1, keepdims=True) + EPSILON)
    unit = projected / length
    query = unit.astype(BF16)
    queries[x, z] = query
    own_q = queries.at[x, z]
    qx = [Group(queries.at[pl.ds(0, 2), pl.ds(0, 4)]) for _ in range(2)]
    query_far = send(own_q, own_q, device(z, x_far, y, c))
    qz = {d: send(own_q, own_q, device((z + d) % 8, x, y, c)) for d in z_order}
    for d in (1, 3):
        qx[0].send(own_q, own_q, device(z, (x + d) % 4, y, c))
    fresh_far.wait_recv()
    block = fresh_all.at[z, x_far]
    fz_far = Group(fresh_all.at[pl.ds(0, 7), x])
    for d in z_order:
        fz_far.send(block, block, device((z + d) % 8, x, y, c))
    fz.wait_recv()
    fresh_line = fresh_all.at[:, x]
    fx = Group(fresh_all.at[:, pl.ds(0, 2)])
    for xx in (x_near, x_back):
        fx.send(fresh_line, fresh_line, device(z, xx, y, c))
    turned = features[...].astype(F32).T
    feat_z[...] = turned.astype(BF16).reshape(8, 64, 128)
    turned = turned.reshape(Z, X, 2, 8, 128)
    for xx in range(X):
        for h in range(2):
            feat_t[xx * 2 + h] = turned[:, xx, h].reshape(Z * 8, 128).astype(BF16)

    up_low.wait_recv()
    far_low = pass_on(down, 0, to_up)
    key_other.send(part(down, 0), part(down, 0), to_other)
    down_high.wait_recv()
    far_high = pass_on(up, 1, to_down)
    key_other.send(part(up, 1), part(up, 1), to_other)
    query_far.wait_recv()
    block = queries.at[x_far, z]
    qz_far = Group(queries.at[x, pl.ds(0, 7)])
    for d in z_order:
        qz_far.send(block, block, device((z + d) % 8, x, y, c))
    for d in z_order:
        qz[d].wait_recv()
        block = queries.at[x, (z + 8 - d) % 8]
        for e in (1, 3):
            qx[z_line.index(d) // 4].send(block, block, device(z, (x + e) % 4, y, c))
    up_high.wait_recv()
    key_other.send(part(down, 1), part(down, 1), to_other)
    down_low.wait_recv()
    key_other.send(part(up, 0), part(up, 0), to_other)
    key_other.wait_recv()

    diagonal = lax.broadcasted_iota(jnp.int32, (ROWS, 128), 0) == lax.broadcasted_iota(
        jnp.int32, (ROWS, 128), 1
    )

    def tile(q, where, num=None, den=None):
        q = q.reshape(Z * ROWS, WIDTH)
        for j in where:
            k = keys[j]
            s = lax.dot_general(q, k, (((1,), (1,)), ((), ())), preferred_element_type=F32)
            e = jnp.exp2(s * SHARP_LOG2E)
            p = jnp.dot(e.astype(BF16), k, preferred_element_type=F32)
            sums = lane_sums(e)
            num = p if num is None else num + p
            den = sums if den is None else den + sums
        return num, den

    def den_rows(den):
        column_sums = jnp.sum(den, axis=1, keepdims=True).reshape(Z, ROWS, 1)
        return jnp.sum(jnp.where(diagonal[None], column_sums, 0.0), axis=1).reshape(Z, 1, 128)

    num_own[...], den_own[...] = tile(queries[x], [yy * 2 + cc for yy in (y, down, up) for cc in (0, 1)])
    far_low.wait_recv()
    far_other = Group(keys.at[0])
    far_other.send(part(far, 0), part(far, 0), to_other)
    far_high.wait_recv()
    far_other.send(part(far, 1), part(far, 1), to_other)

    fz_far.wait_recv()
    fx.wait_recv()
    pos_copy.wait_recv()
    held = fresh_all[...].reshape(Z * X * ROWS, WIDTH)
    lane = lax.broadcasted_iota(jnp.int32, (128, 128), 1)
    first_key = (lax.shift_right_logical(lane, 5) * 256 + (lane & 31) + me_col * ROWS).astype(F32)
    for r in range(2):
        wanted = jnp.broadcast_to(pos_all[r, 0:1, :], (128, 128)).astype(F32).T - first_key
        hits = [jnp.where(wanted == 1024.0 * m, 1.0, 0.0).astype(BF16) for m in range(8)]
        found = jnp.dot(jnp.concatenate(hits, axis=1), held, preferred_element_type=F32)
        found = found.astype(BF16).reshape(4, ROWS, WIDTH)
        for gg in range(4):
            pick_out[((y_hi + r) % 2) * 4 + gg] = found[gg]
    picks = Group(pick_in.at[pl.ds(0, 7)])
    for dy, dc in column:
        yy, cc = (y + dy) % 4, (c + dc) % 2
        picks.send(pick_out.at[yy * 2 + cc], pick_in.at[me_col], device(z, x, yy, cc))
    pick_in[me_col] = pick_out[me_col]

    slot = write_slot[0]

    def window(gg, bb):
        first = (gg * 64 + bb) * SLOT_ROWS - slot
        return first, lax.shift_right_arithmetic(first, 8)

    for target in range(8):
        _, cycle = window(target % 4, z * 8 + x * 2 + target // 4)
        for k in range(3):
            at = jnp.clip(cycle + k, 0, QUERIES // 256 - 1)
            fill_out[target, k] = fresh_all[lax.shift_right_logical(at, 2), at & 3]
    fills = Group(fill_in.at[:, pl.ds(0, 7)])
    for dy, dc in column:
        yy, cc = (y + dy) % 4, (c + dc) % 2
        to = device(z, x, yy, cc)
        fills.send(fill_out.at[yy * 2 + cc], fill_in.at[:, me_col], to)
    fill_in[:, me_col] = fill_out[me_col]

    far_other.wait_recv()
    num_near, den_near = Group(num_in), Group(den_in)

    def near_tile(h):
        qx[h].wait_recv()
        rows = pl.ds(4 * h, 4)
        line = [(z + 8 - d) % 8 for d in z_line[4 * h : 4 * h + 4]]
        q = jnp.concatenate([queries[xx, zz] for xx in (x_back, x_near) for zz in line], axis=0)
        num, den = tile(q, range(8))
        num, den = num.astype(BF16).reshape(Z, ROWS, WIDTH), den_rows(den)
        for i, owner in enumerate((x_back, x_near)):
            to = device(z, owner, y, c)
            num_out[i, rows] = num[4 * i : 4 * i + 4]
            den_out[i, rows] = den[4 * i : 4 * i + 4]
            num_near.send(num_out.at[i, rows], num_in.at[i, rows], to)
            den_near.send(den_out.at[i, rows], den_in.at[i, rows], to)

    near_tile(0)
    qz_far.wait_recv()
    num, den = tile(queries[x_far], range(8))
    num_far_out[...] = num.astype(BF16).reshape(Z, ROWS, WIDTH)
    den_far_out[...] = den_rows(den)
    numf, denf = Group(num_far_in), Group(den_far_in)
    for i, d in enumerate(z_far):
        zz = (z + d) % 8
        to = device(zz, x, y, c)
        denf.send(den_far_out.at[zz], den_far_in.at[i], to)
        numf.send(num_far_out.at[zz], num_far_in.at[i], to)
    near_tile(1)

    num_own[...], den = tile(queries[x], [far * 2, far * 2 + 1], num_own[...], den_own[...])
    den_line[...] = den_rows(den)
    numz, denz = Group(numz_in), Group(denz_in)
    den_near.wait_recv()
    num_near.wait_recv()

    def own_block(d):
        zz, at = (z + d) % 8, z_line.index((8 - d) % 8)
        rows = pl.ds(pl.multiple_of(zz * ROWS, ROWS), ROWS)
        num = num_own[rows] + num_in[0, at].astype(F32) + num_in[1, at].astype(F32)
        return num, den_line[zz] + den_in[0, at] + den_in[1, at]

    for i, d in enumerate(z_far):
        to = device((z + d) % 8, x, y, c)
        num, den = own_block(d)
        numz_out[i], denz_out[i] = num.astype(BF16), den
        numz.send(numz_out.at[i], numz_in.at[i], to)
        denz.send(denz_out.at[i], denz_in.at[i], to)
    denf.wait_recv()
    numf.wait_recv()
    num, den = num_far_out[z].astype(F32), den_far_out[z]
    for i in range(7):
        num = num + num_far_in[i].astype(F32)
        den = den + den_far_in[i]
    num_sum_out[...] = num
    den_sum_out[...] = den
    to = device(z, x_far, y, c)
    den_sum = send(den_sum_out, den_sum_in, to)
    num_sum = send(num_sum_out, num_sum_in, to)

    picks.wait_recv()
    positive = pick_in[0].astype(F32)
    for src in range(1, 8):
        positive = positive + pick_in[src].astype(F32)
    score = SHARP * jnp.sum(query.astype(F32) * positive, axis=1, keepdims=True)
    weight_p = jnp.exp(score)

    numerator, den_row = own_block(0)
    denz.wait_recv()
    numz.wait_recv()
    for i in range(7):
        den_row = den_row + denz_in[i]
        numerator = numerator + numz_in[i].astype(F32)
    den_sum.wait_recv()
    den_row = den_row + den_sum_in[...]
    num_sum.wait_recv()
    numerator = numerator + num_sum_in[...]
    denominator = jnp.sum(
        jnp.where(diagonal, jnp.broadcast_to(den_row, (ROWS, 128)), 0.0),
        axis=1,
        keepdims=True,
    )
    mass = weight_p + denominator
    grad = SHARP * ((weight_p * positive + numerator) / mass - positive)
    along = jnp.sum(grad * unit, axis=1, keepdims=True)
    grad_projected = ((grad - along * unit) / length).astype(BF16)
    gp_all[g] = grad_projected
    gps = Group(gp_all.at[pl.ds(0, 3)])
    for _, yy, cc in group_peers:
        gps.send(gp_all.at[g], gp_all.at[g], device(z, x, yy, cc))
    loss = jnp.log(mass) - score
    place = lax.broadcasted_iota(jnp.int32, (ROWS, 128), 0) + g * ROWS == (
        lax.broadcasted_iota(jnp.int32, (ROWS, 128), 1)
    )
    loss_row = jnp.sum(jnp.where(place, loss, 0.0), axis=0, keepdims=True)
    loss_rows[...] = loss_row
    losses = Group(loss_in)
    for s, yy, cc in group_peers:
        losses.send(loss_rows, loss_in.at[s - 1], device(z, x, yy, cc))
    gps.wait_recv()
    grads = gp_all[...].reshape(128, WIDTH)
    left, right = grads[:, :128], grads[:, 128:]
    wgx, wgz = Group(wgx_in), Group(wgz_in)
    for i, (dx, dy) in enumerate(rect):
        xx, yy = (x + dx) % 4, (y + dy) % 4
        at = xx * 2 + yy // 2
        wgx_out[i] = jnp.dot(feat_t[at], left, preferred_element_type=F32).astype(BF16)
        wgx.send(wgx_out.at[i], wgx_in.at[i], device(z, xx, yy, c))
        zz = (z + z_far[i]) % 8
        wgz_out[i] = jnp.dot(feat_z[zz], right, preferred_element_type=F32).astype(BF16)
        wgz.send(wgz_out.at[i], wgz_in.at[i], device(zz, x, y, c))
    me_rect = x * 2 + y_hi
    wg[0] = jnp.dot(feat_t[me_rect], left, preferred_element_type=F32)
    wg[1] = jnp.dot(feat_z[z], right, preferred_element_type=F32)

    fills.wait_recv()
    first, cycle = window(g, b)
    arrived = fill_in[...].reshape(768, WIDTH)
    row = lax.broadcasted_iota(jnp.int32, (128, 128), 0)
    apart = row - lane + (first - cycle * 256)
    hit = [jnp.where(apart == 128 * m, 1.0, 0.0).astype(BF16) for m in range(3)]
    hit = jnp.concatenate(hit, axis=1)
    place_of = lax.broadcasted_iota(jnp.int32, (128, WIDTH), 0) + first
    for r in range(0, SLOT_ROWS, 128):
        moved = jnp.dot(hit, arrived[r : r + 384], preferred_element_type=F32)
        old = keys[me_col, r : r + 128, :].astype(F32)
        inside = (place_of >= -r) & (place_of < QUERIES - r)
        queue_new[r : r + 128, :] = jnp.where(inside, moved, old).astype(BF16)
    stores = [pltpu.make_async_copy(queue_new, queue_out, local_sem.at[5])]
    stores[0].start()
    losses.wait_recv()
    loss_new[...] = loss_rows[...] + loss_in[0] + loss_in[1] + loss_in[2]
    stores.append(pltpu.make_async_copy(loss_new, loss_out, local_sem.at[6]))
    stores[1].start()

    sums = wg[1]
    wgz.wait_recv()
    for i in range(7):
        sums = sums + wgz_in[i].astype(F32)
    wgx2_out[...] = sums.reshape(8, 8, 128)
    wgx2, wgz2 = Group(wgx2_in), Group(wgz2_in)
    for i, (dx, dy) in enumerate(rect):
        xx, yy = (x + dx) % 4, (y + dy) % 4
        wgx2.send(wgx2_out.at[xx * 2 + yy // 2], wgx2_in.at[i], device(z, xx, yy, c))
    sums = wg[0]
    wgx.wait_recv()
    for i in range(7):
        sums = sums + wgx_in[i].astype(F32)
    wgz2_out[...] = sums.reshape(Z, 8, 128)
    for i, d in enumerate(z_far):
        zz = (z + d) % 8
        wgz2.send(wgz2_out.at[zz], wgz2_in.at[i], device(zz, x, y, c))
    total = wgx2_out[me_rect]
    wgx2.wait_recv()
    for i in range(7):
        total = total + wgx2_in[i]
    wgrad_new[:, 128:] = total
    total = wgz2_out[z]
    wgz2.wait_recv()
    for i in range(7):
        total = total + wgz2_in[i]
    wgrad_new[:, :128] = total
    stores.append(pltpu.make_async_copy(wgrad_new, wgrad_out, local_sem.at[7]))
    stores[2].start()

    assert len(groups) == COPIES
    for i, all_sent in enumerate((sent_large, sent_small)):
        assert sent[i] == math.prod(all_sent.shape) * 4, sent
        pltpu.make_async_remote_copy(
            src_ref=all_sent,
            dst_ref=all_sent,
            send_sem=send_sem.at[i],
            recv_sem=recv_sem.at[0],
            device_id=neighbour,
            device_id_type=pl.DeviceIdType.MESH,
        ).wait_send()
    for copy in stores:
        copy.wait()


def local(features, weight, queue, fresh_keys, positives, write_slot):
    hbm = pl.BlockSpec(memory_space=pltpu.HBM)
    loss, weight_grad, new_queue = pl.pallas_call(
        kernel,
        out_shape=(
            jax.ShapeDtypeStruct((1, 128), F32),
            jax.ShapeDtypeStruct((8, WIDTH), F32),
            jax.ShapeDtypeStruct((SLOT_ROWS, WIDTH), BF16),
        ),
        in_specs=[hbm] * 5 + [pl.BlockSpec(memory_space=pltpu.SMEM)],
        out_specs=(hbm, hbm, hbm),
        scratch_shapes=[
            pltpu.VMEM((128, 512), BF16),
            pltpu.VMEM((512, WIDTH), BF16),
            pltpu.VMEM((4, ROWS, WIDTH), F32),
            pltpu.VMEM((3, ROWS, WIDTH), F32),
            pltpu.VMEM((X, Z, ROWS, WIDTH), BF16),
            pltpu.VMEM((8, SLOT_ROWS, WIDTH), BF16),
            pltpu.VMEM((Z, X, ROWS, WIDTH), BF16),
            pltpu.VMEM((1, 128), jnp.int32),
            pltpu.VMEM((2, 8, 128), jnp.int32),
            pltpu.VMEM((8, ROWS, WIDTH), BF16),
            pltpu.VMEM((8, ROWS, WIDTH), BF16),
            pltpu.VMEM((8, 3, ROWS, WIDTH), BF16),
            pltpu.VMEM((3, 8, ROWS, WIDTH), BF16),
            pltpu.VMEM((8, Z * 8, 128), BF16),
            pltpu.VMEM((8, 64, 128), BF16),
            pltpu.VMEM((Z * ROWS, WIDTH), F32),
            pltpu.VMEM((2, Z, ROWS, WIDTH), BF16),
            pltpu.VMEM((2, Z, ROWS, WIDTH), BF16),
            pltpu.VMEM((Z, ROWS, WIDTH), BF16),
            pltpu.VMEM((7, ROWS, WIDTH), BF16),
            pltpu.VMEM((ROWS, WIDTH), F32),
            pltpu.VMEM((ROWS, WIDTH), F32),
            pltpu.VMEM((7, ROWS, WIDTH), BF16),
            pltpu.VMEM((7, ROWS, WIDTH), BF16),
            pltpu.VMEM((Z * ROWS, 128), F32),
            pltpu.VMEM((2, Z, 1, 128), F32),
            pltpu.VMEM((2, Z, 1, 128), F32),
            pltpu.VMEM((Z, 1, 128), F32),
            pltpu.VMEM((7, 1, 128), F32),
            pltpu.VMEM((1, 128), F32),
            pltpu.VMEM((1, 128), F32),
            pltpu.VMEM((Z, 1, 128), F32),
            pltpu.VMEM((7, 1, 128), F32),
            pltpu.VMEM((7, 1, 128), F32),
            pltpu.VMEM((4, ROWS, WIDTH), BF16),
            pltpu.VMEM((1, 128), F32),
            pltpu.VMEM((3, 1, 128), F32),
            pltpu.VMEM((2, 64, 128), F32),
            pltpu.VMEM((7, 64, 128), BF16),
            pltpu.VMEM((7, 64, 128), BF16),
            pltpu.VMEM((7, 64, 128), BF16),
            pltpu.VMEM((7, 64, 128), BF16),
            pltpu.VMEM((8, 8, 128), F32),
            pltpu.VMEM((7, 8, 128), F32),
            pltpu.VMEM((8, 8, 128), F32),
            pltpu.VMEM((7, 8, 128), F32),
            pltpu.VMEM((SLOT_ROWS, WIDTH), BF16),
            pltpu.VMEM((1, 128), F32),
            pltpu.VMEM((8, WIDTH), F32),
            pltpu.VMEM((LARGE, 8, 128), F32),
            pltpu.VMEM((SMALL, 1, 128), F32),
            pltpu.SemaphoreType.DMA((8,)),
            pltpu.SemaphoreType.DMA((2,)),
            pltpu.SemaphoreType.DMA((COPIES,)),
        ],
        compiler_params=pltpu.CompilerParams(
            collective_id=0, has_side_effects=True, vmem_limit_bytes=60 << 20
        ),
        name="retrieval_step",
    )(features, weight, queue, fresh_keys, positives.reshape(1, 128), write_slot)
    return loss.reshape(128), weight_grad, new_queue


def solution(mesh):
    in_specs = (
        P("blk", "group"),
        P("group", None),
        P(("group", "blk"), None),
        P("blk", None),
        P("blk"),
        P(),
    )
    out_specs = (P("blk"), P(("group", "blk"), None), P(("group", "blk"), None))
    return jax.shard_map(local, mesh=mesh, in_specs=in_specs, out_specs=out_specs, check_vma=False)
```

```python
import functools
import math

import jax
import jax.numpy as jnp
from jax import lax
from jax.experimental import pallas as pl
from jax.experimental.pallas import tpu as pltpu
from jax.sharding import PartitionSpec as P

EPSILON = 1e-06
SHARP = 8.0
SHARP_LOG2E = SHARP * math.log2(math.e)

Z, X, Y, CORES = 8, 4, 4, 2
ROWS = 32
WIDTH = 256
SLOT_ROWS = 512
QUERIES = 8192
F32 = jnp.float32
BF16 = jnp.bfloat16
COPIES = 41
LARGE, SMALL = 1043, 34


def lane_sums(e):
    d = e[:, 0:128]
    for i in range(1, e.shape[1] // 128):
        d = d + e[:, 128 * i : 128 * (i + 1)]
    return d


def kernel(
    features_hbm,
    weight_hbm,
    queue_hbm,
    fresh_hbm,
    positives_hbm,
    write_slot,
    loss_out,
    wgrad_out,
    queue_out,
    features,
    weight,
    proj,
    proj_in,
    queries,
    keys,
    fresh_all,
    pos_row,
    pos_all,
    pick_out,
    pick_in,
    fill_out,
    fill_in,
    feat_t,
    feat_z,
    num_own,
    num_out,
    num_in,
    num_far_out,
    num_far_in,
    num_sum_out,
    num_sum_in,
    numz_out,
    numz_in,
    den_own,
    den_out,
    den_in,
    den_far_out,
    den_far_in,
    den_sum_out,
    den_sum_in,
    den_line,
    denz_out,
    denz_in,
    gp_all,
    loss_rows,
    loss_in,
    wg,
    wgx_out,
    wgx_in,
    wgz_out,
    wgz_in,
    wgx2_out,
    wgx2_in,
    wgz2_out,
    wgz2_in,
    queue_new,
    loss_new,
    wgrad_new,
    sent_large,
    sent_small,
    local_sem,
    send_sem,
    recv_sem,
):
    g = lax.axis_index("group")
    b = lax.axis_index("blk")
    y_lo, c = g // 2, g % 2
    z, x, y_hi = b // 8, (b // 2) % 4, b % 2
    y = 2 * y_hi + y_lo
    me_col = y * 2 + c

    loads = [
        pltpu.make_async_copy(src, dst, local_sem.at[i])
        for i, (src, dst) in enumerate(
            (
                (features_hbm, features),
                (weight_hbm, weight),
                (queue_hbm, keys.at[me_col]),
                (fresh_hbm.at[pl.ds(pl.multiple_of(g * ROWS, ROWS), ROWS)], fresh_all.at[z, x]),
                (positives_hbm, pos_row),
            )
        )
    ]
    for copy in loads:
        copy.start()

    def device(zz, xx, yy, cc):
        return {"group": (yy % 2) * 2 + cc, "blk": zz * 8 + xx * 2 + yy // 2}

    groups, sent = [], [0, 0]

    def small(ref):
        return int(ref.shape[-2] == 1)

    class Group:
        def __init__(self, whole):
            self.at, self.whole, self.got = len(groups), whole, False
            groups.append(self)

        def copy(self, src, dst, to):
            return pltpu.make_async_remote_copy(
                src_ref=src,
                dst_ref=dst,
                send_sem=send_sem.at[small(src)],
                recv_sem=recv_sem.at[self.at],
                device_id=to,
                device_id_type=pl.DeviceIdType.MESH,
            )

        def send(self, src, dst, to):
            sent[small(src)] += math.prod(src.shape) * src.dtype.itemsize
            self.copy(src, dst, to).start()

        def wait_recv(self):
            self.got = True
            self.copy(self.whole, self.whole, neighbour).wait_recv()

    neighbour = device(z, x, y, 1 - c)

    def send(src, dst, to):
        group = Group(src)
        group.send(src, dst, to)
        return group

    column = [(dy, dc) for dy in (0, 1, 3, 2) for dc in (1, 0) if (dy, dc) != (0, 0)]
    z_order = (1, 7, 2, 6, 3, 5, 4)
    z_far = (4, 3, 5, 2, 6, 1, 7)
    z_line = (0, *z_order)
    rect = [(dx, dy) for dx in (2, 1, 3, 0) for dy in (2, 0) if (dx, dy) != (0, 0)]
    x_near, x_far = (x + 1) % 4, (x + 2) % 4
    x_back = (x + 3) % 4

    barrier = pltpu.get_barrier_semaphore()
    peers = [device((z + d) % 8, x, y, c) for d in z_far]
    peers += [device(z, x, (y + dy) % 4, (c + dc) % 2) for dy, dc in column]
    peers += [device(z, (x + dx) % 4, (y + dy) % 4, c) for dx, dy in rect if dx]
    for p in peers:
        pl.semaphore_signal(barrier, inc=1, device_id=p, device_id_type=pl.DeviceIdType.MESH)

    for copy in loads:
        copy.wait()
    proj[...] = jnp.dot(features[...], weight[...], preferred_element_type=F32).reshape(
        4, ROWS, WIDTH
    )
    pos_all[0] = jnp.broadcast_to(pos_row[...], (8, 128))
    pl.semaphore_wait(barrier, len(peers))

    group_peers = []
    for s in (1, 2, 3):
        yy, cc = 2 * y_hi + (y_lo + s // 2) % 2, (c + s % 2) % 2
        group_peers.append((s, yy, cc))
    proj_copies = Group(proj_in)
    for s, yy, cc in group_peers:
        proj_copies.send(proj.at[(yy % 2) * 2 + cc], proj_in.at[s - 1], device(z, x, yy, cc))

    own_f = fresh_all.at[z, x]
    fz = Group(fresh_all.at[pl.ds(0, 7), x])
    fresh_far = send(own_f, own_f, device(z, x_far, y, c))
    for d in z_order:
        fz.send(own_f, own_f, device((z + d) % 8, x, y, c))

    up, down = (y + 1) % 4, (y + 3) % 4
    far = (y + 2) % 4
    other = 1 - c
    to_up, to_down = device(z, x, up, c), device(z, x, down, c)
    to_other = device(z, x, y, other)
    half = SLOT_ROWS // 2

    def part(yy, h):
        return keys.at[yy * 2 + c, pl.ds(h * half, half)]

    def pass_on(yy, h, to):
        return send(part(yy, h), part(yy, h), to)

    up_low = pass_on(y, 0, to_up)
    down_high = pass_on(y, 1, to_down)
    key_other = Group(keys.at[pl.ds(0, 3)])
    for h in range(2):
        key_other.send(part(y, h), part(y, h), to_other)
    up_high = pass_on(y, 1, to_up)
    down_low = pass_on(y, 0, to_down)
    pos_copy = send(pos_all.at[0], pos_all.at[1], device(z, x, far, c))

    proj_copies.wait_recv()
    projected = proj[g] + proj_in[0] + proj_in[1] + proj_in[2]
    length = jnp.sqrt(jnp.sum(projected * projected, axis=1, keepdims=True) + EPSILON)
    unit = projected / length
    query = unit.astype(BF16)
    queries[x, z] = query
    own_q = queries.at[x, z]
    qx = [Group(queries.at[pl.ds(0, 2), pl.ds(0, 4)]) for _ in range(2)]
    query_far = send(own_q, own_q, device(z, x_far, y, c))
    qz = {d: send(own_q, own_q, device((z + d) % 8, x, y, c)) for d in z_order}
    for d in (1, 3):
        qx[0].send(own_q, own_q, device(z, (x + d) % 4, y, c))
    fresh_far.wait_recv()
    block = fresh_all.at[z, x_far]
    fz_far = Group(fresh_all.at[pl.ds(0, 7), x])
    for d in z_order:
        fz_far.send(block, block, device((z + d) % 8, x, y, c))
    fz.wait_recv()
    fresh_line = fresh_all.at[:, x]
    fx = Group(fresh_all.at[:, pl.ds(0, 2)])
    for xx in (x_near, x_back):
        fx.send(fresh_line, fresh_line, device(z, xx, y, c))
    turned = features[...].astype(F32).T
    feat_z[...] = turned.astype(BF16).reshape(8, 64, 128)
    turned = turned.reshape(Z, X, 2, 8, 128)
    for xx in range(X):
        for h in range(2):
            feat_t[xx * 2 + h] = turned[:, xx, h].reshape(Z * 8, 128).astype(BF16)

    up_low.wait_recv()
    far_low = pass_on(down, 0, to_up)
    key_other.send(part(down, 0), part(down, 0), to_other)
    down_high.wait_recv()
    far_high = pass_on(up, 1, to_down)
    key_other.send(part(up, 1), part(up, 1), to_other)
    query_far.wait_recv()
    block = queries.at[x_far, z]
    qz_far = Group(queries.at[x, pl.ds(0, 7)])
    for d in z_order:
        qz_far.send(block, block, device((z + d) % 8, x, y, c))
    for d in z_order:
        qz[d].wait_recv()
        block = queries.at[x, (z + 8 - d) % 8]
        for e in (1, 3):
            qx[z_line.index(d) // 4].send(block, block, device(z, (x + e) % 4, y, c))
    up_high.wait_recv()
    key_other.send(part(down, 1), part(down, 1), to_other)
    down_low.wait_recv()
    key_other.send(part(up, 0), part(up, 0), to_other)
    key_other.wait_recv()

    diagonal = lax.broadcasted_iota(jnp.int32, (ROWS, 128), 0) == lax.broadcasted_iota(
        jnp.int32, (ROWS, 128), 1
    )

    def tile(q, where, num=None, den=None):
        q = q.reshape(Z * ROWS, WIDTH)
        for j in where:
            k = keys[j]
            s = lax.dot_general(q, k, (((1,), (1,)), ((), ())), preferred_element_type=F32)
            e = jnp.exp2(s * SHARP_LOG2E)
            p = jnp.dot(e.astype(BF16), k, preferred_element_type=F32)
            sums = lane_sums(e)
            num = p if num is None else num + p
            den = sums if den is None else den + sums
        return num, den

    def den_rows(den):
        column_sums = jnp.sum(den, axis=1, keepdims=True).reshape(Z, ROWS, 1)
        return jnp.sum(jnp.where(diagonal[None], column_sums, 0.0), axis=1).reshape(Z, 1, 128)

    num_own[...], den_own[...] = tile(queries[x], [yy * 2 + cc for yy in (y, down, up) for cc in (0, 1)])
    far_low.wait_recv()
    far_other = Group(keys.at[0])
    far_other.send(part(far, 0), part(far, 0), to_other)
    far_high.wait_recv()
    far_other.send(part(far, 1), part(far, 1), to_other)

    far_other.wait_recv()
    num_near, den_near = Group(num_in), Group(den_in)

    def near_tile(h):
        qx[h].wait_recv()
        rows = pl.ds(4 * h, 4)
        line = [(z + 8 - d) % 8 for d in z_line[4 * h : 4 * h + 4]]
        q = jnp.concatenate([queries[xx, zz] for xx in (x_back, x_near) for zz in line], axis=0)
        num, den = tile(q, range(8))
        num, den = num.astype(BF16).reshape(Z, ROWS, WIDTH), den_rows(den)
        for i, owner in enumerate((x_back, x_near)):
            to = device(z, owner, y, c)
            num_out[i, rows] = num[4 * i : 4 * i + 4]
            den_out[i, rows] = den[4 * i : 4 * i + 4]
            num_near.send(num_out.at[i, rows], num_in.at[i, rows], to)
            den_near.send(den_out.at[i, rows], den_in.at[i, rows], to)

    near_tile(0)
    qz_far.wait_recv()
    num, den = tile(queries[x_far], range(8))
    num_far_out[...] = num.astype(BF16).reshape(Z, ROWS, WIDTH)
    den_far_out[...] = den_rows(den)
    numf, denf = Group(num_far_in), Group(den_far_in)
    for i, d in enumerate(z_far):
        zz = (z + d) % 8
        to = device(zz, x, y, c)
        denf.send(den_far_out.at[zz], den_far_in.at[i], to)
        numf.send(num_far_out.at[zz], num_far_in.at[i], to)
    near_tile(1)

    num_own[...], den = tile(queries[x], [far * 2, far * 2 + 1], num_own[...], den_own[...])
    den_line[...] = den_rows(den)
    numz, denz = Group(numz_in), Group(denz_in)
    fz_far.wait_recv()
    fx.wait_recv()
    pos_copy.wait_recv()
    held = fresh_all[...].reshape(Z * X * ROWS, WIDTH)
    lane = lax.broadcasted_iota(jnp.int32, (128, 128), 1)
    first_key = (lax.shift_right_logical(lane, 5) * 256 + (lane & 31) + me_col * ROWS).astype(F32)
    for r in range(2):
        wanted = jnp.broadcast_to(pos_all[r, 0:1, :], (128, 128)).astype(F32).T - first_key
        hits = [jnp.where(wanted == 1024.0 * m, 1.0, 0.0).astype(BF16) for m in range(8)]
        found = jnp.dot(jnp.concatenate(hits, axis=1), held, preferred_element_type=F32)
        found = found.astype(BF16).reshape(4, ROWS, WIDTH)
        for gg in range(4):
            pick_out[((y_hi + r) % 2) * 4 + gg] = found[gg]
    picks = Group(pick_in.at[pl.ds(0, 7)])
    for dy, dc in column:
        yy, cc = (y + dy) % 4, (c + dc) % 2
        picks.send(pick_out.at[yy * 2 + cc], pick_in.at[me_col], device(z, x, yy, cc))
    pick_in[me_col] = pick_out[me_col]

    slot = write_slot[0]

    def window(gg, bb):
        first = (gg * 64 + bb) * SLOT_ROWS - slot
        return first, lax.shift_right_arithmetic(first, 8)

    for target in range(8):
        _, cycle = window(target % 4, z * 8 + x * 2 + target // 4)
        for k in range(3):
            at = jnp.clip(cycle + k, 0, QUERIES // 256 - 1)
            fill_out[target, k] = fresh_all[lax.shift_right_logical(at, 2), at & 3]
    fills = Group(fill_in.at[:, pl.ds(0, 7)])
    for dy, dc in column:
        yy, cc = (y + dy) % 4, (c + dc) % 2
        to = device(z, x, yy, cc)
        fills.send(fill_out.at[yy * 2 + cc], fill_in.at[:, me_col], to)
    fill_in[:, me_col] = fill_out[me_col]

    den_near.wait_recv()
    num_near.wait_recv()

    def own_block(d):
        zz, at = (z + d) % 8, z_line.index((8 - d) % 8)
        rows = pl.ds(pl.multiple_of(zz * ROWS, ROWS), ROWS)
        num = num_own[rows] + num_in[0, at].astype(F32) + num_in[1, at].astype(F32)
        return num, den_line[zz] + den_in[0, at] + den_in[1, at]

    for i, d in enumerate(z_far):
        to = device((z + d) % 8, x, y, c)
        num, den = own_block(d)
        numz_out[i], denz_out[i] = num.astype(BF16), den
        numz.send(numz_out.at[i], numz_in.at[i], to)
        denz.send(denz_out.at[i], denz_in.at[i], to)
    denf.wait_recv()
    numf.wait_recv()
    num, den = num_far_out[z].astype(F32), den_far_out[z]
    for i in range(7):
        num = num + num_far_in[i].astype(F32)
        den = den + den_far_in[i]
    num_sum_out[...] = num
    den_sum_out[...] = den
    to = device(z, x_far, y, c)
    den_sum = send(den_sum_out, den_sum_in, to)
    num_sum = send(num_sum_out, num_sum_in, to)

    picks.wait_recv()
    positive = pick_in[0].astype(F32)
    for src in range(1, 8):
        positive = positive + pick_in[src].astype(F32)
    score = SHARP * jnp.sum(query.astype(F32) * positive, axis=1, keepdims=True)
    weight_p = jnp.exp(score)

    numerator, den_row = own_block(0)
    denz.wait_recv()
    numz.wait_recv()
    for i in range(7):
        den_row = den_row + denz_in[i]
        numerator = numerator + numz_in[i].astype(F32)
    den_sum.wait_recv()
    den_row = den_row + den_sum_in[...]
    num_sum.wait_recv()
    numerator = numerator + num_sum_in[...]
    denominator = jnp.sum(
        jnp.where(diagonal, jnp.broadcast_to(den_row, (ROWS, 128)), 0.0),
        axis=1,
        keepdims=True,
    )
    mass = weight_p + denominator
    grad = SHARP * ((weight_p * positive + numerator) / mass - positive)
    along = jnp.sum(grad * unit, axis=1, keepdims=True)
    grad_projected = ((grad - along * unit) / length).astype(BF16)
    gp_all[g] = grad_projected
    gps = Group(gp_all.at[pl.ds(0, 3)])
    for _, yy, cc in group_peers:
        gps.send(gp_all.at[g], gp_all.at[g], device(z, x, yy, cc))
    loss = jnp.log(mass) - score
    place = lax.broadcasted_iota(jnp.int32, (ROWS, 128), 0) + g * ROWS == (
        lax.broadcasted_iota(jnp.int32, (ROWS, 128), 1)
    )
    loss_row = jnp.sum(jnp.where(place, loss, 0.0), axis=0, keepdims=True)
    loss_rows[...] = loss_row
    losses = Group(loss_in)
    for s, yy, cc in group_peers:
        losses.send(loss_rows, loss_in.at[s - 1], device(z, x, yy, cc))
    gps.wait_recv()
    grads = gp_all[...].reshape(128, WIDTH)
    left, right = grads[:, :128], grads[:, 128:]
    wgx, wgz = Group(wgx_in), Group(wgz_in)
    for i, (dx, dy) in enumerate(rect):
        xx, yy = (x + dx) % 4, (y + dy) % 4
        at = xx * 2 + yy // 2
        wgx_out[i] = jnp.dot(feat_t[at], left, preferred_element_type=F32).astype(BF16)
        wgx.send(wgx_out.at[i], wgx_in.at[i], device(z, xx, yy, c))
        zz = (z + z_far[i]) % 8
        wgz_out[i] = jnp.dot(feat_z[zz], right, preferred_element_type=F32).astype(BF16)
        wgz.send(wgz_out.at[i], wgz_in.at[i], device(zz, x, y, c))
    me_rect = x * 2 + y_hi
    wg[0] = jnp.dot(feat_t[me_rect], left, preferred_element_type=F32)
    wg[1] = jnp.dot(feat_z[z], right, preferred_element_type=F32)

    fills.wait_recv()
    first, cycle = window(g, b)
    arrived = fill_in[...].reshape(768, WIDTH)
    row = lax.broadcasted_iota(jnp.int32, (128, 128), 0)
    apart = row - lane + (first - cycle * 256)
    hit = [jnp.where(apart == 128 * m, 1.0, 0.0).astype(BF16) for m in range(3)]
    hit = jnp.concatenate(hit, axis=1)
    place_of = lax.broadcasted_iota(jnp.int32, (128, WIDTH), 0) + first
    for r in range(0, SLOT_ROWS, 128):
        moved = jnp.dot(hit, arrived[r : r + 384], preferred_element_type=F32)
        old = keys[me_col, r : r + 128, :].astype(F32)
        inside = (place_of >= -r) & (place_of < QUERIES - r)
        queue_new[r : r + 128, :] = jnp.where(inside, moved, old).astype(BF16)
    stores = [pltpu.make_async_copy(queue_new, queue_out, local_sem.at[5])]
    stores[0].start()
    losses.wait_recv()
    loss_new[...] = loss_rows[...] + loss_in[0] + loss_in[1] + loss_in[2]
    stores.append(pltpu.make_async_copy(loss_new, loss_out, local_sem.at[6]))
    stores[1].start()

    sums = wg[1]
    wgz.wait_recv()
    for i in range(7):
        sums = sums + wgz_in[i].astype(F32)
    wgx2_out[...] = sums.reshape(8, 8, 128)
    wgx2, wgz2 = Group(wgx2_in), Group(wgz2_in)
    for i, (dx, dy) in enumerate(rect):
        xx, yy = (x + dx) % 4, (y + dy) % 4
        wgx2.send(wgx2_out.at[xx * 2 + yy // 2], wgx2_in.at[i], device(z, xx, yy, c))
    sums = wg[0]
    wgx.wait_recv()
    for i in range(7):
        sums = sums + wgx_in[i].astype(F32)
    wgz2_out[...] = sums.reshape(Z, 8, 128)
    for i, d in enumerate(z_far):
        zz = (z + d) % 8
        wgz2.send(wgz2_out.at[zz], wgz2_in.at[i], device(zz, x, y, c))
    total = wgx2_out[me_rect]
    wgx2.wait_recv()
    for i in range(7):
        total = total + wgx2_in[i]
    wgrad_new[:, 128:] = total
    total = wgz2_out[z]
    wgz2.wait_recv()
    for i in range(7):
        total = total + wgz2_in[i]
    wgrad_new[:, :128] = total
    stores.append(pltpu.make_async_copy(wgrad_new, wgrad_out, local_sem.at[7]))
    stores[2].start()

    assert len(groups) == COPIES
    for i, all_sent in enumerate((sent_large, sent_small)):
        assert sent[i] == math.prod(all_sent.shape) * 4, sent
        pltpu.make_async_remote_copy(
            src_ref=all_sent,
            dst_ref=all_sent,
            send_sem=send_sem.at[i],
            recv_sem=recv_sem.at[0],
            device_id=neighbour,
            device_id_type=pl.DeviceIdType.MESH,
        ).wait_send()
    for copy in stores:
        copy.wait()


def local(features, weight, queue, fresh_keys, positives, write_slot):
    hbm = pl.BlockSpec(memory_space=pltpu.HBM)
    loss, weight_grad, new_queue = pl.pallas_call(
        kernel,
        out_shape=(
            jax.ShapeDtypeStruct((1, 128), F32),
            jax.ShapeDtypeStruct((8, WIDTH), F32),
            jax.ShapeDtypeStruct((SLOT_ROWS, WIDTH), BF16),
        ),
        in_specs=[hbm] * 5 + [pl.BlockSpec(memory_space=pltpu.SMEM)],
        out_specs=(hbm, hbm, hbm),
        scratch_shapes=[
            pltpu.VMEM((128, 512), BF16),
            pltpu.VMEM((512, WIDTH), BF16),
            pltpu.VMEM((4, ROWS, WIDTH), F32),
            pltpu.VMEM((3, ROWS, WIDTH), F32),
            pltpu.VMEM((X, Z, ROWS, WIDTH), BF16),
            pltpu.VMEM((8, SLOT_ROWS, WIDTH), BF16),
            pltpu.VMEM((Z, X, ROWS, WIDTH), BF16),
            pltpu.VMEM((1, 128), jnp.int32),
            pltpu.VMEM((2, 8, 128), jnp.int32),
            pltpu.VMEM((8, ROWS, WIDTH), BF16),
            pltpu.VMEM((8, ROWS, WIDTH), BF16),
            pltpu.VMEM((8, 3, ROWS, WIDTH), BF16),
            pltpu.VMEM((3, 8, ROWS, WIDTH), BF16),
            pltpu.VMEM((8, Z * 8, 128), BF16),
            pltpu.VMEM((8, 64, 128), BF16),
            pltpu.VMEM((Z * ROWS, WIDTH), F32),
            pltpu.VMEM((2, Z, ROWS, WIDTH), BF16),
            pltpu.VMEM((2, Z, ROWS, WIDTH), BF16),
            pltpu.VMEM((Z, ROWS, WIDTH), BF16),
            pltpu.VMEM((7, ROWS, WIDTH), BF16),
            pltpu.VMEM((ROWS, WIDTH), F32),
            pltpu.VMEM((ROWS, WIDTH), F32),
            pltpu.VMEM((7, ROWS, WIDTH), BF16),
            pltpu.VMEM((7, ROWS, WIDTH), BF16),
            pltpu.VMEM((Z * ROWS, 128), F32),
            pltpu.VMEM((2, Z, 1, 128), F32),
            pltpu.VMEM((2, Z, 1, 128), F32),
            pltpu.VMEM((Z, 1, 128), F32),
            pltpu.VMEM((7, 1, 128), F32),
            pltpu.VMEM((1, 128), F32),
            pltpu.VMEM((1, 128), F32),
            pltpu.VMEM((Z, 1, 128), F32),
            pltpu.VMEM((7, 1, 128), F32),
            pltpu.VMEM((7, 1, 128), F32),
            pltpu.VMEM((4, ROWS, WIDTH), BF16),
            pltpu.VMEM((1, 128), F32),
            pltpu.VMEM((3, 1, 128), F32),
            pltpu.VMEM((2, 64, 128), F32),
            pltpu.VMEM((7, 64, 128), BF16),
            pltpu.VMEM((7, 64, 128), BF16),
            pltpu.VMEM((7, 64, 128), BF16),
            pltpu.VMEM((7, 64, 128), BF16),
            pltpu.VMEM((8, 8, 128), F32),
            pltpu.VMEM((7, 8, 128), F32),
            pltpu.VMEM((8, 8, 128), F32),
            pltpu.VMEM((7, 8, 128), F32),
            pltpu.VMEM((SLOT_ROWS, WIDTH), BF16),
            pltpu.VMEM((1, 128), F32),
            pltpu.VMEM((8, WIDTH), F32),
            pltpu.VMEM((LARGE, 8, 128), F32),
            pltpu.VMEM((SMALL, 1, 128), F32),
            pltpu.SemaphoreType.DMA((8,)),
            pltpu.SemaphoreType.DMA((2,)),
            pltpu.SemaphoreType.DMA((COPIES,)),
        ],
        compiler_params=pltpu.CompilerParams(
            collective_id=0, has_side_effects=True, vmem_limit_bytes=60 << 20
        ),
        name="retrieval_step",
    )(features, weight, queue, fresh_keys, positives.reshape(1, 128), write_slot)
    return loss.reshape(128), weight_grad, new_queue


def solution(mesh):
    in_specs = (
        P("blk", "group"),
        P("group", None),
        P(("group", "blk"), None),
        P("blk", None),
        P("blk"),
        P(),
    )
    out_specs = (P("blk"), P(("group", "blk"), None), P(("group", "blk"), None))
    return jax.shard_map(local, mesh=mesh, in_specs=in_specs, out_specs=out_specs, check_vma=False)
```
